128 devices in a mesh: clip: 32 (over z, x, y_lo), group: 4 (over y_hi, core).
Axes of the slice: x: 4, y: 4 (y_hi: 2, y_lo: 2; y = y_hi * 2 + y_lo), z: 4, core: 2. Of those that a mesh axis runs over, the one named last changes fastest.
Arguments:
- clip_frames: bfloat16 [4, 32, 64, 64, 256], P('group', 'clip'), may hold values from -6 to 6
- w_spatial: bfloat16 [3, 3, 256, 256], replicated, may hold values from -0.125 to 0.125
- w_time: bfloat16 [3, 256, 256], replicated, may hold values from -0.21875 to 0.21875
- cotangent: bfloat16 [4, 16, 64, 64, 256], P('group', None, 'clip'), may hold values from -6 to 6
- frame_time: int32 [32], replicated, may hold values from 0 to 31, each once
Outputs:
- clip_grad: bfloat16 [4, 32, 64, 64, 256], P('group', 'clip')
- space_grad: float32 [3, 3, 256, 256], P(None, None, None, 'group')
- time_grad: float32 [3, 256, 256], P(None, None, 'group')
The draws below stay inside these ranges and needn't reach their ends.
Inputs may be any that keep to these rules, and one draw needn't show every extreme that they name: `frame_time`: each time from 0 to 31 appears exactly once, the same table for every clip.
All inputs are finite; a program needn't handle non-finite values.
Results may differ from the reference program's by a relative error of at most 0.0058.
Values may be sent and summed in bfloat16 or wider, within the bound.
No kernel may reach another device: no remote copies, remote signals or barrier semaphores. Data moves between devices by JAX's collectives and lax.ppermute only.
A program may use at most 128 MiB of HBM per device.

```python
import math
import jax
import jax.numpy as jnp
import numpy as np
from jax import lax

C = 256
W_CELLS = 64
FRAMES = 32
HALF = 16
HEIGHT = 64
CLIPS = 4


def steps_of(key, shape, cuts, smallest, top_value):
    loudness, own = 1.0, jax.random.fold_in(key, 6)
    for axis_at, parts in cuts:
        draws = jnp.exp(jax.random.uniform(jax.random.fold_in(own, axis_at), (parts,), jnp.float32, smallest / len(cuts), top_value / len(cuts)))
        loudness = loudness * jnp.repeat(draws, shape[axis_at] // parts).reshape([-1 if axis == axis_at else 1 for axis in range(len(shape))])
    return loudness


def normal_values(own_key, dims, scale, reach, shards=(), dtype=jnp.bfloat16):
    gain = steps_of(own_key, dims, shards, -0.22, 0.18) if shards else 1.0
    entries = jax.random.normal(own_key, dims, jnp.float32) * scale * gain
    return jnp.minimum(jnp.maximum(entries, -reach), reach).astype(dtype)


def setup_inputs(seed: int = 0) -> dict:
    seeds = jax.random.split(jax.random.key(seed), 6)
    return {
        "clip_frames": normal_values(seeds[0], (CLIPS, FRAMES, HEIGHT, W_CELLS, C), 1.0, 6.0, ((0, 4), (1, 32))),
        "w_spatial": normal_values(seeds[1], (3, 3, C, C), (9 * C) ** -0.5, 0.125),
        "w_time": normal_values(seeds[2], (3, C, C), (3 * C) ** -0.5, 0.21875),
        "cotangent": normal_values(seeds[3], (CLIPS, HALF, HEIGHT, W_CELLS, C), 1.0, 6.0, ((0, 4), (2, 32))),
        "frame_time": jax.random.permutation(seeds[4], FRAMES).astype(jnp.int32),
    }


def conv_forward(frames, weight):
    height = frames.shape[1]
    col_count = frames.shape[2]
    padded = jnp.pad(frames, ((0, 0), (1, 1), (1, 1), (0, 0)))
    running = jnp.zeros(frames.shape, jnp.float32)
    for row_tap in range(3):
        for col_tap in range(3):
            window = padded[:, row_tap:row_tap + height, col_tap:col_tap + col_count].astype(jnp.float32)
            running = running + jnp.einsum('fhwc,cd->fhwd', window, weight[row_tap, col_tap].astype(jnp.float32))
    return running

def conv_transpose(grads, weight):
    height = grads.shape[1]
    col_count = grads.shape[2]
    padded = jnp.pad(grads, ((0, 0), (1, 1), (1, 1), (0, 0)))
    running = jnp.zeros(grads.shape, jnp.float32)
    for row_tap in range(3):
        for col_tap in range(3):
            window = padded[:, 2 - row_tap:2 - row_tap + height, 2 - col_tap:2 - col_tap + col_count].astype(jnp.float32)
            running = running + jnp.einsum('fhwd,cd->fhwc', window, weight[row_tap, col_tap].astype(jnp.float32))
    return running

def filter_grad(frames, grads):
    height = frames.shape[1]
    col_count = frames.shape[2]
    padded = jnp.pad(frames, ((0, 0), (1, 1), (1, 1), (0, 0)))
    rows_out = []
    for row_tap in range(3):
        taps = []
        for col_tap in range(3):
            window = padded[:, row_tap:row_tap + height, col_tap:col_tap + col_count].astype(jnp.float32)
            taps.append(jnp.einsum('fhwc,fhwd->cd', window, grads.astype(jnp.float32)))
        rows_out.append(jnp.stack(taps))
    return jnp.stack(rows_out)

def silu_slope(values):
    sig = jax.nn.sigmoid(values)
    return sig * (1.0 + values * (1.0 - sig))

def time_tables(frame_count, half_count):
    places = np.arange(frame_count)
    lead_index = places // 2
    odd_flag = places % 2 == 1
    trail_index = np.minimum((places + 1) // 2, half_count - 1)
    trail_valid = odd_flag & ((places + 1) // 2 < half_count) | (places == 0)
    even_mask = (~odd_flag).astype(np.float32)
    return (lead_index, trail_index, trail_valid, even_mask)

def temporal(acts, lead_part, trail_part, w_time, even_mask):
    w_lead = jnp.where(even_mask[:, None, None] > 0.5, w_time[1], w_time[2])
    grads = jnp.einsum('fhwd,fcd->fhwc', lead_part.astype(jnp.float32), w_lead.astype(jnp.float32))
    grads = grads + jnp.einsum('fhwd,cd->fhwc', trail_part.astype(jnp.float32), w_time[0].astype(jnp.float32))
    per_frame = jnp.einsum('fhwc,fhwd->fcd', acts.astype(jnp.float32), lead_part.astype(jnp.float32))
    grad_one = jnp.einsum('f,fcd->cd', even_mask, per_frame)
    grad_two = jnp.einsum('f,fcd->cd', 1.0 - even_mask, per_frame)
    grad_zero = jnp.einsum('fhwc,fhwd->cd', acts.astype(jnp.float32), trail_part.astype(jnp.float32))
    return (grads.astype(jnp.bfloat16), jnp.stack([grad_zero, grad_one, grad_two]))

def reference(clip_frames, w_spatial, w_time, cotangent, frame_time):
    lead_index, trail_index, trail_valid, even_np = time_tables(FRAMES, HALF)
    even_mask = jnp.asarray(even_np, jnp.float32)
    inverse = jnp.argsort(frame_time).astype(jnp.int32)

    def one_clip(inputs):
        frames, cotan = inputs
        hidden = conv_forward(frames, w_spatial)
        acts = jax.nn.silu(hidden).astype(jnp.bfloat16)
        acts_time = acts[inverse]
        lead_part = cotan[jnp.asarray(lead_index, jnp.int32)]
        trail_part = jnp.where(jnp.asarray(trail_valid)[:, None, None, None], cotan[jnp.asarray(trail_index, jnp.int32)], jnp.zeros((), jnp.bfloat16)).astype(jnp.bfloat16)
        grad_time, wt_grad = temporal(acts_time, lead_part, trail_part, w_time, even_mask)
        grad_acts = grad_time[frame_time]
        hidden_grad = (grad_acts.astype(jnp.float32) * silu_slope(hidden)).astype(jnp.bfloat16)
        ws_grad = filter_grad(frames, hidden_grad)
        clip_grad = conv_transpose(hidden_grad, w_spatial).astype(jnp.bfloat16)
        return (clip_grad, ws_grad, wt_grad)
    clip_grad, ws_all, wt_all = lax.map(one_clip, (clip_frames, cotangent))
    factor = 1.0 / math.sqrt(CLIPS * FRAMES * HEIGHT * W_CELLS)
    space_grad = lax.optimization_barrier(jnp.sum(ws_all, axis=0)) * factor
    time_grad = lax.optimization_barrier(jnp.sum(wt_all, axis=0)) * factor
    return (clip_grad, space_grad, time_grad)
```

```python
import functools
import math

import jax
import jax.numpy as jnp
from jax import lax
from jax.experimental import pallas as pl
from jax.experimental.pallas import tpu as pltpu
from jax.sharding import PartitionSpec as P

BF16 = jnp.bfloat16
F32 = jnp.float32
VMEM_LIMIT = 48 * 1024 * 1024
BOTH = ("clip", "group")


def dot(a, b, dims=((1,), (0,))):
    return lax.dot_general(a, b, (dims, ((), ())), preferred_element_type=F32)


def params():
    return pltpu.CompilerParams(vmem_limit_bytes=VMEM_LIMIT)


def vmem():
    return pl.BlockSpec(memory_space=pltpu.VMEM)


def smem():
    return pl.BlockSpec(memory_space=pltpu.SMEM)


def cost(flops, nbytes, trans=0):
    return pl.CostEstimate(flops=flops, bytes_accessed=nbytes, transcendentals=trans)


def place_of_time(frame_time, inverse):
    def put(s, carry):
        inverse[frame_time[s]] = s
        return carry

    lax.fori_loop(0, frame_time.shape[0], put, 0)


def time_grad_kernel(frame_time, cot, w_time, out, inverse):
    half, pixels, chans = cot.shape
    place_of_time(frame_time, inverse)
    span = min(4, half)
    across = ((1,), (1,))
    for first in range(0, half, span):
        here = cot[first : first + span].reshape(span * pixels, chans)
        even = dot(here, w_time[1], across)
        odd = dot(here, w_time[2], across)
        if first + span < half:
            after = cot[first + 1 : first + span + 1].reshape(span * pixels, chans)
        else:
            after = jnp.concatenate(
                [cot[first + 1 : half].reshape((span - 1) * pixels, chans), jnp.zeros((pixels, chans), BF16)]
            )
        odd = odd + dot(after, w_time[0], across)
        for k in range(span):
            part = even[k * pixels : (k + 1) * pixels]
            if first + k == 0:
                part = part + dot(cot[0], w_time[0], across)
            out[inverse[2 * (first + k)]] = part.astype(BF16)
            out[inverse[2 * (first + k) + 1]] = odd[k * pixels : (k + 1) * pixels].astype(BF16)


def time_grad_call(frame_time, cot, w_time):
    half, pixels, chans = cot.shape
    count = frame_time.shape[0]
    return pl.pallas_call(
        time_grad_kernel,
        out_shape=jax.ShapeDtypeStruct((count, pixels, chans), BF16),
        in_specs=[smem(), vmem(), vmem()],
        out_specs=vmem(),
        scratch_shapes=[pltpu.SMEM((count,), jnp.int32)],
        compiler_params=params(),
        cost_estimate=cost(6 * half * pixels * chans * chans, 4 * count * pixels * chans),
        name="time_grad",
    )(frame_time, cot, w_time)


def side_by_side(block, width):
    rows, chans = block.shape
    wide = block.astype(F32)
    col = lax.rem(lax.broadcasted_iota(jnp.int32, (rows, chans), 0), width)
    left = jnp.where(col == 0, 0.0, pltpu.roll(wide, 1, 0)).astype(BF16)
    right = jnp.where(col == width - 1, 0.0, pltpu.roll(wide, rows - 1, 0)).astype(BF16)
    return left, block, right


def store_cat(cat, start, block, width):
    rows, chans = block.shape
    for j, part in enumerate(side_by_side(block, width)):
        cat[pl.ds(start, rows), j * chans : (j + 1) * chans] = part


def forward_kernel(width, x, w, acts, slope, cat):
    step = pl.program_id(0)
    pixels, chans = x.shape
    rows = acts.shape[0]

    @pl.when(step == 0)
    def _():
        cat[0:width] = jnp.zeros((width, 3 * chans), BF16)
        cat[width + pixels :] = jnp.zeros((width, 3 * chans), BF16)

        def fill(k, carry):
            at = pl.multiple_of(k * rows, rows)
            store_cat(cat, width + at, x[pl.ds(at, rows)], width)
            return carry

        lax.fori_loop(0, pixels // rows, fill, 0)

    at = pl.multiple_of(step * rows, rows)
    hidden = dot(cat[pl.ds(at, rows)], w[0])
    hidden = hidden + dot(cat[pl.ds(at + width, rows)], w[1])
    hidden = hidden + dot(cat[pl.ds(at + 2 * width, rows)], w[2])
    sig = 1.0 / (1.0 + jnp.exp(-hidden))
    acts[...] = (hidden * sig).astype(BF16)
    slope[...] = sig * (1.0 + hidden * (1.0 - sig))


def forward_call(x, w, width, steps=8):
    pixels, chans = x.shape
    rows = pixels // steps
    whole = lambda shape: pl.BlockSpec(shape, lambda k: (0,) * len(shape))
    tile = pl.BlockSpec((rows, chans), lambda k: (k, 0))
    return pl.pallas_call(
        functools.partial(forward_kernel, width),
        grid=(steps,),
        out_shape=(jax.ShapeDtypeStruct((pixels, chans), BF16), jax.ShapeDtypeStruct((pixels, chans), F32)),
        in_specs=[whole(x.shape), whole(w.shape)],
        out_specs=(tile, tile),
        scratch_shapes=[pltpu.VMEM((pixels + 2 * width, 3 * chans), BF16)],
        compiler_params=params(),
        cost_estimate=cost(18 * pixels * chans * chans, 8 * pixels * chans, 2 * pixels * chans),
        name="spatial_forward",
    )(x, w)


def filter_kernel(width, grad, slope, xt, hidden_grad, ws, cat, total):
    step = pl.program_id(0)
    last = pl.num_programs(0) - 1
    rows, chans = grad.shape
    pixels = rows * last

    @pl.when(step == 0)
    def _():
        cat[0:width] = jnp.zeros((width, 3 * chans), BF16)
        cat[width + pixels :] = jnp.zeros((width, 3 * chans), BF16)
        total[...] = jnp.zeros_like(total)

    @pl.when(step < last)
    def _():
        at = pl.multiple_of(step * rows, rows)
        block = (grad[...].astype(F32) * slope[...]).astype(BF16)
        hidden_grad[...] = block
        store_cat(cat, width + at, block, width)

    @pl.when(step > 0)
    def _():
        at = pl.multiple_of((step - 1) * rows, rows)
        for i in range(3):
            total[i] += dot(xt[...], cat[pl.ds(at + (2 - i) * width, rows)])

    @pl.when(step == last)
    def _():
        for i in range(3):
            for j in range(3):
                ws[i, j] = total[i, :, (2 - j) * chans : (3 - j) * chans].T


def filter_call(grad, slope, xt, width, steps=8):
    pixels, chans = grad.shape
    rows = pixels // steps
    tile = pl.BlockSpec((rows, chans), lambda k: (jnp.minimum(k, steps - 1), 0))
    return pl.pallas_call(
        functools.partial(filter_kernel, width),
        grid=(steps + 1,),
        out_shape=(
            jax.ShapeDtypeStruct((pixels, chans), BF16),
            jax.ShapeDtypeStruct((3, 3, chans, chans), F32),
        ),
        in_specs=[tile, tile, pl.BlockSpec((chans, rows), lambda k: (0, jnp.maximum(k - 1, 0)))],
        out_specs=(tile, pl.BlockSpec((3, 3, chans, chans), lambda k: (0, 0, 0, 0))),
        scratch_shapes=[
            pltpu.VMEM((pixels + 2 * width, 3 * chans), BF16),
            pltpu.VMEM((3, chans, 3 * chans), F32),
        ],
        compiler_params=params(),
        cost_estimate=cost(18 * pixels * chans * chans, 12 * pixels * chans),
        name="spatial_filter",
    )(grad, slope, xt)


def back_kernel(width, hidden_grad, w, out, cat):
    step = pl.program_id(0)
    pixels, chans = hidden_grad.shape
    rows = out.shape[0]

    @pl.when(step == 0)
    def _():
        cat[0:width] = jnp.zeros((width, 3 * chans), BF16)
        cat[width + pixels :] = jnp.zeros((width, 3 * chans), BF16)

        def fill(k, carry):
            at = pl.multiple_of(k * rows, rows)
            store_cat(cat, width + at, hidden_grad[pl.ds(at, rows)], width)
            return carry

        lax.fori_loop(0, pixels // rows, fill, 0)

    at = pl.multiple_of(step * rows, rows)
    total = dot(cat[pl.ds(at, rows)], w[0])
    total = total + dot(cat[pl.ds(at + width, rows)], w[1])
    total = total + dot(cat[pl.ds(at + 2 * width, rows)], w[2])
    out[...] = total.astype(BF16)


def back_call(hidden_grad, w, width, steps=8):
    pixels, chans = hidden_grad.shape
    rows = pixels // steps
    whole = lambda shape: pl.BlockSpec(shape, lambda k: (0,) * len(shape))
    return pl.pallas_call(
        functools.partial(back_kernel, width),
        grid=(steps,),
        out_shape=jax.ShapeDtypeStruct((pixels, chans), BF16),
        in_specs=[whole(hidden_grad.shape), whole(w.shape)],
        out_specs=pl.BlockSpec((rows, chans), lambda k: (k, 0)),
        scratch_shapes=[pltpu.VMEM((pixels + 2 * width, 3 * chans), BF16)],
        compiler_params=params(),
        cost_estimate=cost(18 * pixels * chans * chans, 4 * pixels * chans),
        name="spatial_back",
    )(hidden_grad, w)


def time_filter_kernel(frame_time, acts, cot_t, wt, inverse):
    count, pixels, chans = acts.shape
    half = count // 2
    place_of_time(frame_time, inverse)
    first = acts[inverse[0]]
    totals = [dot(cot_t[:, 0:pixels], first), None, None]
    totals[1] = totals[0]
    for u in range(half):
        here = cot_t[:, u * pixels : (u + 1) * pixels]
        if u > 0:
            totals[1] = totals[1] + dot(here, acts[inverse[2 * u]])
        odd = acts[inverse[2 * u + 1]]
        term = dot(here, odd)
        totals[2] = term if totals[2] is None else totals[2] + term
        if u + 1 < half:
            totals[0] = totals[0] + dot(cot_t[:, (u + 1) * pixels : (u + 2) * pixels], odd)
    for k in range(3):
        wt[k] = totals[k]


def time_filter_call(frame_time, acts, cot_t):
    count, pixels, chans = acts.shape
    return pl.pallas_call(
        time_filter_kernel,
        out_shape=jax.ShapeDtypeStruct((3, chans, chans), F32),
        in_specs=[smem(), vmem(), vmem()],
        out_specs=vmem(),
        scratch_shapes=[pltpu.SMEM((count,), jnp.int32)],
        compiler_params=params(),
        cost_estimate=cost(3 * count * pixels * chans * chans, 3 * count * pixels * chans),
        name="time_filter",
    )(frame_time, acts, cot_t)


def exchange(x, axes):
    return lax.all_to_all(x, axes, split_axis=0, concat_axis=0, tiled=True)


def local(clip_frames, w_spatial, w_time, cotangent, frame_time):
    count = frame_time.shape[0]
    height, width, chans = clip_frames.shape[2:]
    clips = lax.axis_size("clip")
    groups = lax.axis_size("group")
    share = chans // groups
    x = clip_frames.reshape(height * width, chans)
    cot = cotangent.reshape(count // 2, -1, chans)

    grad = exchange(time_grad_call(frame_time, cot, w_time), "clip")
    acts, slope = forward_call(x, w_spatial.reshape(3, 3 * chans, chans), width)
    rows_acts = exchange(acts.reshape(count, -1, chans), "clip")
    w_back = w_spatial[::-1, ::-1].transpose(0, 1, 3, 2).reshape(3, 3 * chans, chans)
    hidden_grad, ws = filter_call(grad.reshape(height * width, chans), slope, x.T, width)
    clip_grad = back_call(hidden_grad, w_back, width)
    wt = time_filter_call(frame_time, rows_acts, cot.transpose(2, 0, 1).reshape(chans, -1))

    parts = jnp.concatenate([ws.reshape(9, chans, chans), wt]).astype(BF16)
    taps = parts.shape[0]
    depth = taps * share // clips
    parts = parts.reshape(taps, groups, share, chans).transpose(1, 0, 2, 3)
    parts = parts.reshape(groups, clips, depth, chans).transpose(1, 0, 2, 3)
    parts = exchange(parts.reshape(clips * groups, depth, chans), BOTH)
    clip_total = clip_frames.shape[0] * groups
    factor = 1.0 / math.sqrt(clip_total * count * height * width)
    mine = (jnp.sum(parts.astype(F32), axis=0) * factor).astype(BF16)
    full = exchange(jnp.broadcast_to(mine[None], (clips, depth, chans)), "clip")
    full = full.reshape(taps, share, chans).transpose(0, 2, 1).astype(F32)
    return (clip_grad.reshape(clip_frames.shape), full[:9].reshape(3, 3, chans, share), full[9:])


def solution(mesh):
    return jax.shard_map(
        local,
        mesh=mesh,
        in_specs=(
            P("group", "clip", None, None, None),
            P(),
            P(),
            P("group", None, "clip", None, None),
            P(),
        ),
        out_specs=(
            P("group", "clip", None, None, None),
            P(None, None, None, "group"),
            P(None, None, "group"),
        ),
        check_vma=False,
    )
```

```python
import functools
import math

import jax
import jax.numpy as jnp
from jax import lax
from jax.experimental import pallas as pl
from jax.experimental.pallas import tpu as pltpu
from jax.sharding import Mesh
from jax.sharding import PartitionSpec as P

BF16 = jnp.bfloat16
F32 = jnp.float32


def dot(a, b, dims=((1,), (0,))):
    return lax.dot_general(a, b, (dims, ((), ())), preferred_element_type=F32)


def params(mib=24):
    return pltpu.CompilerParams(vmem_limit_bytes=mib * 1024 * 1024)


def vmem():
    return pl.BlockSpec(memory_space=pltpu.VMEM)


def hbm():
    return pl.BlockSpec(memory_space=pltpu.HBM)


def smem():
    return pl.BlockSpec(memory_space=pltpu.SMEM)


def far(x):
    return pltpu.with_memory_space_constraint(x, pltpu.HBM)


def cost(flops, nbytes, trans=0):
    return pl.CostEstimate(flops=flops, bytes_accessed=nbytes, transcendentals=trans)


def spread_kernel(times, cot, out, frame_time, held, load, sent):
    half = held.shape[0]
    fetch = pltpu.make_async_copy(cot, held, load.at[0])
    order = pltpu.make_async_copy(times, frame_time, load.at[1])
    fetch.start()
    order.start()
    order.wait()
    fetch.wait()

    def send(s, carry):
        t = frame_time[s]
        pltpu.make_async_copy(held.at[t // 2], out.at[s, 0], sent).start()
        pltpu.make_async_copy(held.at[jnp.minimum((t + 1) // 2, half - 1)], out.at[s, 1], sent).start()
        return carry

    lax.fori_loop(0, out.shape[0], send, 0)
    pltpu.make_async_copy(out, out, sent).wait()


def spread_call(frame_time, cot):
    half, pixels, chans = cot.shape
    count = frame_time.shape[0]
    return pl.pallas_call(
        spread_kernel,
        out_shape=jax.ShapeDtypeStruct((count, 2, pixels, chans), BF16),
        in_specs=[hbm(), hbm()],
        out_specs=hbm(),
        scratch_shapes=[
            pltpu.SMEM((count,), jnp.int32),
            pltpu.VMEM((half, pixels, chans), BF16),
            pltpu.SemaphoreType.DMA((2,)),
            pltpu.SemaphoreType.DMA,
        ],
        compiler_params=params(60),
        cost_estimate=cost(0, 10 * half * pixels * chans),
        name="spread",
    )(frame_time, cot)


def side_by_side(block, width):
    rows, chans = block.shape
    wide = block.astype(F32)
    col = lax.rem(lax.broadcasted_iota(jnp.int32, (rows, chans), 0), width)
    left = jnp.where(col == 0, 0.0, pltpu.roll(wide, 1, 0)).astype(BF16)
    right = jnp.where(col == width - 1, 0.0, pltpu.roll(wide, rows - 1, 0)).astype(BF16)
    return left, block, right


def store_cat(cat, start, block, width):
    rows, chans = block.shape
    for j, part in enumerate(side_by_side(block, width)):
        cat[pl.ds(start, rows), j * chans : (j + 1) * chans] = part


def forward_kernel(width, x, w, acts, slope, cat):
    step = pl.program_id(0)
    pixels, chans = x.shape
    rows = acts.shape[0]

    @pl.when(step == 0)
    def _():
        cat[0:width] = jnp.zeros((width, 3 * chans), BF16)
        cat[width + pixels :] = jnp.zeros((width, 3 * chans), BF16)

        def fill(k, carry):
            at = pl.multiple_of(k * rows, rows)
            store_cat(cat, width + at, x[pl.ds(at, rows)], width)
            return carry

        lax.fori_loop(0, pixels // rows, fill, 0)

    at = pl.multiple_of(step * rows, rows)
    hidden = dot(cat[pl.ds(at, rows)], w[0])
    hidden = hidden + dot(cat[pl.ds(at + width, rows)], w[1])
    hidden = hidden + dot(cat[pl.ds(at + 2 * width, rows)], w[2])
    sig = 1.0 / (1.0 + jnp.exp(-hidden))
    acts[...] = (hidden * sig).astype(BF16)
    slope[...] = sig * (1.0 + hidden * (1.0 - sig))


def forward_call(x, w, width, steps=4):
    pixels, chans = x.shape
    rows = pixels // steps
    whole = lambda shape: pl.BlockSpec(shape, lambda k: (0,) * len(shape))
    tile = pl.BlockSpec((rows, chans), lambda k: (k, 0))
    return pl.pallas_call(
        functools.partial(forward_kernel, width),
        grid=(steps,),
        out_shape=(jax.ShapeDtypeStruct((pixels, chans), BF16), jax.ShapeDtypeStruct((pixels, chans), F32)),
        in_specs=[whole(x.shape), whole(w.shape)],
        out_specs=(tile, tile),
        scratch_shapes=[pltpu.VMEM((pixels + 2 * width, 3 * chans), BF16)],
        compiler_params=params(),
        cost_estimate=cost(18 * pixels * chans * chans, 8 * pixels * chans, 2 * pixels * chans),
        name="spatial_forward",
    )(x, w)


def filter_kernel(
    width, cuts, place, recv, slope_in, acts_in, frames_in, padded_in, w_time_in, hidden_grad, keep, send,
    w_time_t, lead, trail, slope, acts_t, frames_t, padded_t, hidden, ws, wt, arrived, left
):
    pixels, chans = slope.shape
    tile_pixels = recv.shape[2]
    edge = 2 * width

    def fetch(k):
        start, stop = cuts[k], cuts[k + 1]
        at = pl.ds(start, stop - start)
        those = pl.ds(start // tile_pixels, (stop - start) // tile_pixels)
        late = start + edge if k else 0
        beyond = pl.ds(late, stop + edge - late)
        pairs = (
            (recv.at[those, 0], lead.at[those]),
            (recv.at[those, 1], trail.at[those]),
            (slope_in.at[at], slope.at[at]),
            (acts_in.at[:, at], acts_t.at[:, at]),
            (frames_in.at[:, at], frames_t.at[:, at]),
            (padded_in.at[:, beyond], padded_t.at[:, beyond]),
        )
        return [pltpu.make_async_copy(a, b, arrived.at[k, n]) for n, (a, b) in enumerate(pairs)]

    copies = [fetch(k) for k in range(len(cuts) - 1)]
    copies[0].append(pltpu.make_async_copy(w_time_in, w_time_t, arrived.at[0, 6]))
    for copy in copies[0]:
        copy.start()

    time, core, count = place[0], place[1], place[2]
    even = lax.rem(time, 2) == 0
    has_trail = jnp.where(even, time == 0, time < count - 1)
    trail_weight = jnp.where(has_trail, 1.0, 0.0)

    def add(total, rows, at, first, term):
        rows = slice(rows * chans, (rows + 1) * chans)
        total[rows, at] = term if first else total[rows, at] + term

    leaving = []
    for k, start in enumerate(cuts[:-1]):
        stop = cuts[k + 1]
        at, those = slice(start, stop), slice(start // tile_pixels, stop // tile_pixels)
        for copy in copies[k]:
            copy.wait()
        if k == 0:
            w_lead = w_time_t[jnp.where(even, 1, 2)]
            w_trail = (w_time_t[0].astype(F32) * trail_weight).astype(BF16)
        for copy in copies[k + 1] if k + 2 < len(cuts) else ():
            copy.start()
        lead_tile = lead[those].reshape(stop - start, chans)
        trail_tile = trail[those].reshape(stop - start, chans)
        grad = (dot(lead_tile, w_lead) + dot(trail_tile, w_trail)).astype(BF16)
        block = (grad.astype(F32) * slope[at]).astype(BF16)
        hidden[at] = block
        span = pl.ds(start, stop - start)
        leaving.append(pltpu.make_async_copy(hidden.at[span], hidden_grad.at[span], left.at[k]))
        leaving[-1].start()
        add(wt, 0, slice(0, chans), k == 0, dot(acts_t[:, at], trail_tile))
        add(wt, 0, slice(chans, 2 * chans), k == 0, dot(acts_t[:, at], lead_tile))
        right = jnp.concatenate(side_by_side(block, width)[::-1], axis=1)
        above, below = padded_t[:, at], padded_t[:, start + edge : stop + edge]
        for i, rows in enumerate((above, frames_t[:, at], below)):
            add(ws, i, slice(None), k == 0, dot(rows, right))

    share = chans // 4

    def put(tap, block):
        turned = block.T
        for half in range(2):
            at = (half * 12 + tap) * share
            one = turned[2 * half * share : (2 * half + 1) * share]
            two = turned[(2 * half + 1) * share : (2 * half + 2) * share]
            keep[at : at + share] = jnp.where(core == 0, one, two)
            send[at : at + share] = jnp.where(core == 0, two, one).astype(BF16)

    for i in range(3):
        for j in range(3):
            put(3 * i + j, ws[i * chans : (i + 1) * chans, j * chans : (j + 1) * chans])
    put(9, wt[:, 0:chans] * trail_weight)
    put(10, wt[:, chans : 2 * chans] * jnp.where(even, 1.0, 0.0))
    put(11, wt[:, chans : 2 * chans] * jnp.where(even, 0.0, 1.0))
    for copy in leaving:
        copy.wait()


def filter_call(place, recv, slope, acts_t, frames_t, padded_t, w_time_t, width, pieces=(1, 1, 1, 1)):
    pixels, chans = slope.shape
    count, _, tile_pixels, _ = recv.shape
    half = (6 * chans, chans)
    cuts = [pixels * sum(pieces[:k]) // sum(pieces) for k in range(len(pieces) + 1)]
    return pl.pallas_call(
        functools.partial(filter_kernel, width, cuts),
        out_shape=(
            jax.ShapeDtypeStruct((pixels, chans), BF16),
            pltpu.VMEM(half, F32),
            pltpu.VMEM(half, BF16),
        ),
        in_specs=[smem()] + [hbm()] * 6,
        out_specs=(hbm(), vmem(), vmem()),
        scratch_shapes=[
            pltpu.VMEM(w_time_t.shape, BF16),
            pltpu.VMEM((count, tile_pixels, chans), BF16),
            pltpu.VMEM((count, tile_pixels, chans), BF16),
            pltpu.VMEM((pixels, chans), F32),
            pltpu.VMEM((chans, pixels), BF16),
            pltpu.VMEM((chans, pixels), BF16),
            pltpu.VMEM((chans, pixels + 2 * width), BF16),
            pltpu.VMEM((pixels, chans), BF16),
            pltpu.VMEM((3 * chans, 3 * chans), F32),
            pltpu.VMEM((chans, 2 * chans), F32),
            pltpu.SemaphoreType.DMA((len(pieces), 7)),
            pltpu.SemaphoreType.DMA((len(pieces),)),
        ],
        compiler_params=params(40),
        cost_estimate=cost(26 * pixels * chans * chans, 18 * pixels * chans),
        name="filters",
    )(place, *(far(x) for x in (recv, slope, acts_t, frames_t, padded_t, w_time_t)))


def back_kernel(width, hidden_grad, w, out, cat):
    step = pl.program_id(0)
    pixels, chans = hidden_grad.shape
    rows = out.shape[0]

    @pl.when(step == 0)
    def _():
        cat[0:width] = jnp.zeros((width, 3 * chans), BF16)
        cat[width + pixels :] = jnp.zeros((width, 3 * chans), BF16)

        def fill(k, carry):
            at = pl.multiple_of(k * rows, rows)
            store_cat(cat, width + at, hidden_grad[pl.ds(at, rows)], width)
            return carry

        lax.fori_loop(0, pixels // rows, fill, 0)

    at = pl.multiple_of(step * rows, rows)
    total = dot(cat[pl.ds(at, rows)], w[0])
    total = total + dot(cat[pl.ds(at + width, rows)], w[1])
    total = total + dot(cat[pl.ds(at + 2 * width, rows)], w[2])
    out[...] = total.astype(BF16)


def back_call(hidden_grad, w, width, steps=4):
    pixels, chans = hidden_grad.shape
    rows = pixels // steps
    whole = lambda shape: pl.BlockSpec(shape, lambda k: (0,) * len(shape))
    return pl.pallas_call(
        functools.partial(back_kernel, width),
        grid=(steps,),
        out_shape=jax.ShapeDtypeStruct((pixels, chans), BF16),
        in_specs=[whole(hidden_grad.shape), whole(w.shape)],
        out_specs=pl.BlockSpec((rows, chans), lambda k: (k, 0)),
        scratch_shapes=[pltpu.VMEM((pixels + 2 * width, 3 * chans), BF16)],
        compiler_params=params(),
        cost_estimate=cost(18 * pixels * chans * chans, 4 * pixels * chans),
        name="spatial_back",
    )(hidden_grad, w)


def total_kernel(factor, parts, out):
    def add(k, total):
        return total + parts[k].astype(F32)

    total = lax.fori_loop(1, parts.shape[0], add, parts[0].astype(F32), unroll=True)
    mine = (total * factor).astype(BF16)
    for k in range(out.shape[0]):
        out[k] = mine


def total_call(parts, factor, copies):
    sources, depth, chans = parts.shape
    return pl.pallas_call(
        functools.partial(total_kernel, factor),
        out_shape=jax.ShapeDtypeStruct((copies, depth, chans), BF16),
        in_specs=[vmem()],
        out_specs=vmem(),
        compiler_params=params(),
        cost_estimate=cost(sources * depth * chans, 3 * sources * depth * chans),
        name="total",
    )(parts)


def turn_kernel(rows, ws, wt):
    taps = ws.shape[0] + wt.shape[0]
    share = rows.shape[0] // taps
    for tap in range(taps):
        block = rows[tap * share : (tap + 1) * share].astype(F32)
        if tap < ws.shape[0]:
            ws[tap] = block
        else:
            wt[tap - ws.shape[0]] = block


def turn_call(rows, share):
    chans = rows.shape[1]
    return pl.pallas_call(
        turn_kernel,
        out_shape=(jax.ShapeDtypeStruct((9, share, chans), F32), jax.ShapeDtypeStruct((3, share, chans), F32)),
        in_specs=[vmem()],
        out_specs=(vmem(), vmem()),
        compiler_params=params(),
        cost_estimate=cost(0, 6 * rows.shape[0] * chans),
        name="turn",
    )(rows)


def exchange(x, axes):
    return lax.all_to_all(x, axes, split_axis=0, concat_axis=0, tiled=True)


def local(clip_frames, w_spatial, w_time, cotangent, frame_time):
    count = frame_time.shape[0]
    height, width, chans = clip_frames.shape[2:]
    pixels = height * width
    clips = lax.axis_size("clip")
    groups = lax.axis_size("half") * lax.axis_size("core")
    share = chans // groups
    x = clip_frames.reshape(pixels, chans)

    recv = exchange(spread_call(frame_time, cotangent.reshape(count // 2, -1, chans)), "clip")
    acts, slope = forward_call(x, w_spatial.reshape(3, 3 * chans, chans), width)
    padded_t = jnp.pad(x.T, ((0, 0), (width, width)))
    place = jnp.stack([frame_time[lax.axis_index("clip")], lax.axis_index("core"), jnp.int32(count)])
    hidden_grad, keep, send = filter_call(
        place, recv, slope, acts.T, x.T, padded_t, w_time.transpose(0, 2, 1), width
    )
    w_back = w_spatial[::-1, ::-1].transpose(0, 1, 3, 2).reshape(3, 3 * chans, chans)
    clip_grad = back_call(hidden_grad, w_back, width)

    came = lax.ppermute(send, "core", [(0, 1), (1, 0)])
    depth = keep.shape[0] // (2 * clips)
    parts = (keep + came.astype(F32)).astype(BF16).reshape(2 * clips, depth, chans)
    parts = exchange(parts, ("half", "clip"))
    factor = 1.0 / math.sqrt(clip_frames.shape[0] * groups * count * pixels)
    rows = exchange(total_call(parts, factor, clips), "clip")
    ws, wt = turn_call(rows.reshape(clips * depth, chans), share)
    ws = ws.reshape(3, 3, share, chans).transpose(0, 1, 3, 2)
    return (clip_grad.reshape(clip_frames.shape), ws, wt.transpose(0, 2, 1))


def solution(mesh):
    clips, groups = mesh.devices.shape
    parts = Mesh(mesh.devices.reshape(clips, 2, groups // 2), ("clip", "half", "core"))
    group = ("half", "core")
    return jax.shard_map(
        local,
        mesh=parts,
        in_specs=(
            P(group, "clip", None, None, None),
            P(),
            P(),
            P(group, None, "clip", None, None),
            P(),
        ),
        out_specs=(
            P(group, "clip", None, None, None),
            P(None, None, None, group),
            P(None, None, group),
        ),
        check_vma=False,
    )
```

```python
import functools
import math

import jax
import jax.numpy as jnp
from jax import lax
from jax.experimental import pallas as pl
from jax.experimental.pallas import tpu as pltpu
from jax.sharding import Mesh
from jax.sharding import PartitionSpec as P

BF16 = jnp.bfloat16
F32 = jnp.float32


def dot(a, b, dims=((1,), (0,))):
    return lax.dot_general(a, b, (dims, ((), ())), preferred_element_type=F32)


def params(mib=24):
    return pltpu.CompilerParams(vmem_limit_bytes=mib * 1024 * 1024)


def vmem():
    return pl.BlockSpec(memory_space=pltpu.VMEM)


def hbm():
    return pl.BlockSpec(memory_space=pltpu.HBM)


def smem():
    return pl.BlockSpec(memory_space=pltpu.SMEM)


def far(x):
    return pltpu.with_memory_space_constraint(x, pltpu.HBM)


def cost(flops, nbytes, trans=0):
    return pl.CostEstimate(flops=flops, bytes_accessed=nbytes, transcendentals=trans)


def spread_kernel(times, cot, out, frame_time, held, load, sent):
    half = held.shape[0]
    fetch = pltpu.make_async_copy(cot, held, load.at[0])
    order = pltpu.make_async_copy(times, frame_time, load.at[1])
    fetch.start()
    order.start()
    order.wait()
    fetch.wait()

    def send(s, carry):
        t = frame_time[s]
        pltpu.make_async_copy(held.at[t // 2], out.at[s, 0], sent).start()
        pltpu.make_async_copy(held.at[jnp.minimum((t + 1) // 2, half - 1)], out.at[s, 1], sent).start()
        return carry

    lax.fori_loop(0, out.shape[0], send, 0)
    pltpu.make_async_copy(out, out, sent).wait()


def spread_call(frame_time, cot):
    half, pixels, chans = cot.shape
    count = frame_time.shape[0]
    return pl.pallas_call(
        spread_kernel,
        out_shape=jax.ShapeDtypeStruct((count, 2, pixels, chans), BF16),
        in_specs=[hbm(), hbm()],
        out_specs=hbm(),
        scratch_shapes=[
            pltpu.SMEM((count,), jnp.int32),
            pltpu.VMEM((half, pixels, chans), BF16),
            pltpu.SemaphoreType.DMA((2,)),
            pltpu.SemaphoreType.DMA,
        ],
        compiler_params=params(60),
        cost_estimate=cost(0, 10 * half * pixels * chans),
        name="spread",
    )(frame_time, cot)


def side_by_side(block, width):
    rows, chans = block.shape
    wide = block.astype(F32)
    col = lax.rem(lax.broadcasted_iota(jnp.int32, (rows, chans), 0), width)
    left = jnp.where(col == 0, 0.0, pltpu.roll(wide, 1, 0)).astype(BF16)
    right = jnp.where(col == width - 1, 0.0, pltpu.roll(wide, rows - 1, 0)).astype(BF16)
    return left, block, right


def store_cat(cat, start, block, width):
    rows, chans = block.shape
    for j, part in enumerate(side_by_side(block, width)):
        cat[pl.ds(start, rows), j * chans : (j + 1) * chans] = part


def forward_kernel(width, x, w, acts, slope, cat):
    step = pl.program_id(0)
    pixels, chans = x.shape
    rows = acts.shape[0]

    @pl.when(step == 0)
    def _():
        cat[0:width] = jnp.zeros((width, 3 * chans), BF16)
        cat[width + pixels :] = jnp.zeros((width, 3 * chans), BF16)

        def fill(k, carry):
            at = pl.multiple_of(k * rows, rows)
            store_cat(cat, width + at, x[pl.ds(at, rows)], width)
            return carry

        lax.fori_loop(0, pixels // rows, fill, 0)

    at = pl.multiple_of(step * rows, rows)
    hidden = dot(cat[pl.ds(at, rows)], w[0])
    hidden = hidden + dot(cat[pl.ds(at + width, rows)], w[1])
    hidden = hidden + dot(cat[pl.ds(at + 2 * width, rows)], w[2])
    sig = 1.0 / (1.0 + jnp.exp(-hidden))
    acts[...] = (hidden * sig).astype(BF16)
    slope[...] = sig * (1.0 + hidden * (1.0 - sig))


def forward_call(x, w, width, steps=4):
    pixels, chans = x.shape
    rows = pixels // steps
    whole = lambda shape: pl.BlockSpec(shape, lambda k: (0,) * len(shape))
    tile = pl.BlockSpec((rows, chans), lambda k: (k, 0))
    return pl.pallas_call(
        functools.partial(forward_kernel, width),
        grid=(steps,),
        out_shape=(jax.ShapeDtypeStruct((pixels, chans), BF16), jax.ShapeDtypeStruct((pixels, chans), F32)),
        in_specs=[whole(x.shape), whole(w.shape)],
        out_specs=(tile, tile),
        scratch_shapes=[pltpu.VMEM((pixels + 2 * width, 3 * chans), BF16)],
        compiler_params=params(),
        cost_estimate=cost(18 * pixels * chans * chans, 8 * pixels * chans, 2 * pixels * chans),
        name="spatial_forward",
    )(x, w)


def filter_kernel(
    width, cuts, place, recv, slope_in, acts_in, frames_in, padded_in, w_time_in, hidden_grad, keep, send,
    w_time_t, lead, trail, slope, acts_t, frames_t, padded_t, hidden, ws, wt, arrived, left
):
    pixels, chans = slope.shape
    tile_pixels = recv.shape[2]
    edge = 2 * width

    def fetch(k):
        start, stop = cuts[k], cuts[k + 1]
        at = pl.ds(start, stop - start)
        those = pl.ds(start // tile_pixels, (stop - start) // tile_pixels)
        late = start + edge if k else 0
        beyond = pl.ds(late, stop + edge - late)
        pairs = (
            (recv.at[those, 0], lead.at[those]),
            (recv.at[those, 1], trail.at[those]),
            (slope_in.at[at], slope.at[at]),
            (acts_in.at[:, at], acts_t.at[:, at]),
            (frames_in.at[:, at], frames_t.at[:, at]),
            (padded_in.at[:, beyond], padded_t.at[:, beyond]),
        )
        return [pltpu.make_async_copy(a, b, arrived.at[k, n]) for n, (a, b) in enumerate(pairs)]

    copies = [fetch(k) for k in range(len(cuts) - 1)]
    copies[0].append(pltpu.make_async_copy(w_time_in, w_time_t, arrived.at[0, 6]))
    for copy in copies[0]:
        copy.start()

    time, core, count = place[0], place[1], place[2]
    even = lax.rem(time, 2) == 0
    has_trail = jnp.where(even, time == 0, time < count - 1)
    trail_weight = jnp.where(has_trail, 1.0, 0.0)

    def add(total, rows, at, first, term):
        rows = slice(rows * chans, (rows + 1) * chans)
        total[rows, at] = term if first else total[rows, at] + term

    leaving = []
    for k, start in enumerate(cuts[:-1]):
        stop = cuts[k + 1]
        at, those = slice(start, stop), slice(start // tile_pixels, stop // tile_pixels)
        for copy in copies[k]:
            copy.wait()
        if k == 0:
            w_lead = w_time_t[jnp.where(even, 1, 2)]
            w_trail = (w_time_t[0].astype(F32) * trail_weight).astype(BF16)
        for copy in copies[k + 1] if k + 2 < len(cuts) else ():
            copy.start()
        lead_tile = lead[those].reshape(stop - start, chans)
        trail_tile = trail[those].reshape(stop - start, chans)
        grad = (dot(lead_tile, w_lead) + dot(trail_tile, w_trail)).astype(BF16)
        block = (grad.astype(F32) * slope[at]).astype(BF16)
        hidden[at] = block
        span = pl.ds(start, stop - start)
        leaving.append(pltpu.make_async_copy(hidden.at[span], hidden_grad.at[span], left.at[k]))
        leaving[-1].start()
        add(wt, 0, slice(0, chans), k == 0, dot(acts_t[:, at], trail_tile))
        add(wt, 0, slice(chans, 2 * chans), k == 0, dot(acts_t[:, at], lead_tile))
        right = jnp.concatenate(side_by_side(block, width)[::-1], axis=1)
        above, below = padded_t[:, at], padded_t[:, start + edge : stop + edge]
        for i, rows in enumerate((above, frames_t[:, at], below)):
            add(ws, i, slice(None), k == 0, dot(rows, right))

    share = chans // 4

    def put(tap, block):
        turned = block.T
        for half in range(2):
            at = (half * 12 + tap) * share
            one = turned[2 * half * share : (2 * half + 1) * share]
            two = turned[(2 * half + 1) * share : (2 * half + 2) * share]
            keep[at : at + share] = jnp.where(core == 0, one, two)
            send[at : at + share] = jnp.where(core == 0, two, one).astype(BF16)

    for i in range(3):
        for j in range(3):
            put(3 * i + j, ws[i * chans : (i + 1) * chans, j * chans : (j + 1) * chans])
    put(9, wt[:, 0:chans] * trail_weight)
    put(10, wt[:, chans : 2 * chans] * jnp.where(even, 1.0, 0.0))
    put(11, wt[:, chans : 2 * chans] * jnp.where(even, 0.0, 1.0))
    for copy in leaving:
        copy.wait()


def filter_call(place, recv, slope, acts_t, frames_t, padded_t, w_time_t, width, pieces=(1, 1, 1, 1)):
    pixels, chans = slope.shape
    count, _, tile_pixels, _ = recv.shape
    half = (6 * chans, chans)
    cuts = [pixels * sum(pieces[:k]) // sum(pieces) for k in range(len(pieces) + 1)]
    return pl.pallas_call(
        functools.partial(filter_kernel, width, cuts),
        out_shape=(
            jax.ShapeDtypeStruct((pixels, chans), BF16),
            pltpu.VMEM(half, F32),
            pltpu.VMEM(half, BF16),
        ),
        in_specs=[smem()] + [hbm()] * 6,
        out_specs=(hbm(), vmem(), vmem()),
        scratch_shapes=[
            pltpu.VMEM(w_time_t.shape, BF16),
            pltpu.VMEM((count, tile_pixels, chans), BF16),
            pltpu.VMEM((count, tile_pixels, chans), BF16),
            pltpu.VMEM((pixels, chans), F32),
            pltpu.VMEM((chans, pixels), BF16),
            pltpu.VMEM((chans, pixels), BF16),
            pltpu.VMEM((chans, pixels + 2 * width), BF16),
            pltpu.VMEM((pixels, chans), BF16),
            pltpu.VMEM((3 * chans, 3 * chans), F32),
            pltpu.VMEM((chans, 2 * chans), F32),
            pltpu.SemaphoreType.DMA((len(pieces), 7)),
            pltpu.SemaphoreType.DMA((len(pieces),)),
        ],
        compiler_params=params(40),
        cost_estimate=cost(26 * pixels * chans * chans, 18 * pixels * chans),
        name="filters",
    )(place, *(far(x) for x in (recv, slope, acts_t, frames_t, padded_t, w_time_t)))


def back_kernel(width, hidden_grad, w, out, cat):
    step = pl.program_id(0)
    pixels, chans = hidden_grad.shape
    rows = out.shape[0]

    @pl.when(step == 0)
    def _():
        cat[0:width] = jnp.zeros((width, 3 * chans), BF16)
        cat[width + pixels :] = jnp.zeros((width, 3 * chans), BF16)

        def fill(k, carry):
            at = pl.multiple_of(k * rows, rows)
            store_cat(cat, width + at, hidden_grad[pl.ds(at, rows)], width)
            return carry

        lax.fori_loop(0, pixels // rows, fill, 0)

    at = pl.multiple_of(step * rows, rows)
    total = dot(cat[pl.ds(at, rows)], w[0])
    total = total + dot(cat[pl.ds(at + width, rows)], w[1])
    total = total + dot(cat[pl.ds(at + 2 * width, rows)], w[2])
    out[...] = total.astype(BF16)


def back_call(hidden_grad, w, width, steps=4):
    pixels, chans = hidden_grad.shape
    rows = pixels // steps
    whole = lambda shape: pl.BlockSpec(shape, lambda k: (0,) * len(shape))
    return pl.pallas_call(
        functools.partial(back_kernel, width),
        grid=(steps,),
        out_shape=jax.ShapeDtypeStruct((pixels, chans), BF16),
        in_specs=[whole(hidden_grad.shape), whole(w.shape)],
        out_specs=pl.BlockSpec((rows, chans), lambda k: (k, 0)),
        scratch_shapes=[pltpu.VMEM((pixels + 2 * width, 3 * chans), BF16)],
        compiler_params=params(),
        cost_estimate=cost(18 * pixels * chans * chans, 4 * pixels * chans),
        name="spatial_back",
    )(hidden_grad, w)


def total_kernel(factor, parts, out):
    def add(k, total):
        return total + parts[k].astype(F32)

    total = lax.fori_loop(1, parts.shape[0], add, parts[0].astype(F32), unroll=True)
    mine = (total * factor).astype(BF16)
    for k in range(out.shape[0]):
        out[k] = mine


def total_call(parts, factor, copies):
    sources, depth, chans = parts.shape
    return pl.pallas_call(
        functools.partial(total_kernel, factor),
        out_shape=jax.ShapeDtypeStruct((copies, depth, chans), BF16),
        in_specs=[vmem()],
        out_specs=vmem(),
        compiler_params=params(),
        cost_estimate=cost(sources * depth * chans, 3 * sources * depth * chans),
        name="total",
    )(parts)


def turn_kernel(rows, ws, wt):
    taps = ws.shape[0] + wt.shape[0]
    share = rows.shape[0] // taps
    for tap in range(taps):
        block = rows[tap * share : (tap + 1) * share].astype(F32)
        if tap < ws.shape[0]:
            ws[tap] = block
        else:
            wt[tap - ws.shape[0]] = block


def turn_call(rows, share):
    chans = rows.shape[1]
    return pl.pallas_call(
        turn_kernel,
        out_shape=(jax.ShapeDtypeStruct((9, share, chans), F32), jax.ShapeDtypeStruct((3, share, chans), F32)),
        in_specs=[vmem()],
        out_specs=(vmem(), vmem()),
        compiler_params=params(),
        cost_estimate=cost(0, 6 * rows.shape[0] * chans),
        name="turn",
    )(rows)


def exchange(x, axes):
    return lax.all_to_all(x, axes, split_axis=0, concat_axis=0, tiled=True)


def local(clip_frames, w_spatial, w_time, cotangent, frame_time):
    count = frame_time.shape[0]
    height, width, chans = clip_frames.shape[2:]
    pixels = height * width
    clips = lax.axis_size("clip")
    groups = lax.axis_size("half") * lax.axis_size("core")
    share = chans // groups
    x = clip_frames.reshape(pixels, chans)

    recv = exchange(spread_call(frame_time, cotangent.reshape(count // 2, -1, chans)), "clip")
    acts, slope = forward_call(x, w_spatial.reshape(3, 3 * chans, chans), width)
    padded_t = jnp.pad(x.T, ((0, 0), (width, width)))
    place = jnp.stack([frame_time[lax.axis_index("clip")], lax.axis_index("core"), jnp.int32(count)])
    hidden_grad, keep, send = filter_call(
        place, recv, slope, acts.T, x.T, padded_t, w_time.transpose(0, 2, 1), width
    )
    w_back = w_spatial[::-1, ::-1].transpose(0, 1, 3, 2).reshape(3, 3 * chans, chans)
    clip_grad = back_call(hidden_grad, w_back, width)

    came = lax.ppermute(send, "core", [(0, 1), (1, 0)])
    depth = keep.shape[0] // (2 * clips)
    parts = (keep + came.astype(F32)).astype(BF16).reshape(2 * clips, depth, chans)
    parts = exchange(parts, ("half", "clip"))
    parts, clip_grad = lax.optimization_barrier((parts, clip_grad))
    factor = 1.0 / math.sqrt(clip_frames.shape[0] * groups * count * pixels)
    rows = exchange(total_call(parts, factor, clips), "clip")
    ws, wt = turn_call(rows.reshape(clips * depth, chans), share)
    ws = ws.reshape(3, 3, share, chans).transpose(0, 1, 3, 2)
    return (clip_grad.reshape(clip_frames.shape), ws, wt.transpose(0, 2, 1))


def solution(mesh):
    clips, groups = mesh.devices.shape
    parts = Mesh(mesh.devices.reshape(clips, 2, groups // 2), ("clip", "half", "core"))
    group = ("half", "core")
    return jax.shard_map(
        local,
        mesh=parts,
        in_specs=(
            P(group, "clip", None, None, None),
            P(),
            P(),
            P(group, None, "clip", None, None),
            P(),
        ),
        out_specs=(
            P(group, "clip", None, None, None),
            P(None, None, None, group),
            P(None, None, group),
        ),
        check_vma=False,
    )
```

```python
import functools
import math

import jax
import jax.numpy as jnp
from jax import lax
from jax.experimental import pallas as pl
from jax.experimental.pallas import tpu as pltpu
from jax.sharding import Mesh
from jax.sharding import PartitionSpec as P

SPREAD = 4
BF16 = jnp.bfloat16
F32 = jnp.float32


def dot(a, b, dims=((1,), (0,))):
    return lax.dot_general(a, b, (dims, ((), ())), preferred_element_type=F32)


def params(mib=24):
    return pltpu.CompilerParams(vmem_limit_bytes=mib * 1024 * 1024)


def vmem():
    return pl.BlockSpec(memory_space=pltpu.VMEM)


def hbm():
    return pl.BlockSpec(memory_space=pltpu.HBM)


def smem():
    return pl.BlockSpec(memory_space=pltpu.SMEM)


def far(x):
    return pltpu.with_memory_space_constraint(x, pltpu.HBM)


def cost(flops, nbytes, trans=0):
    return pl.CostEstimate(flops=flops, bytes_accessed=nbytes, transcendentals=trans)


def spread_kernel(times, cot, out, frame_time, place, held, load, sent):
    half = held.shape[0]
    count = out.shape[0]
    order = pltpu.make_async_copy(times, frame_time, load.at[0])
    order.start()
    span = half // (load.shape[0] - 1)
    pieces = []
    for k in range(load.shape[0] - 1):
        at = pl.ds(k * span, span)
        pieces.append(pltpu.make_async_copy(cot.at[at], held.at[at], load.at[k + 1]))
        pieces[-1].start()
    order.wait()

    def put(s, carry):
        place[frame_time[s]] = s
        return carry

    lax.fori_loop(0, count, put, 0)
    for k, piece in enumerate(pieces):
        piece.wait()
        for u in range(k * span, (k + 1) * span):
            leads = (2 * u, 2 * u + 1)
            trails = tuple(t for t in range(count) if min((t + 1) // 2, half - 1) == u)
            for which, wanted in enumerate((leads, trails)):
                for t in wanted:
                    pltpu.make_async_copy(held.at[u], out.at[place[t], which], sent).start()
    pltpu.make_async_copy(out, out, sent).wait()


def spread_call(frame_time, cot):
    half, pixels, chans = cot.shape
    count = frame_time.shape[0]
    return pl.pallas_call(
        spread_kernel,
        out_shape=jax.ShapeDtypeStruct((count, 2, pixels, chans), BF16),
        in_specs=[hbm(), hbm()],
        out_specs=hbm(),
        scratch_shapes=[
            pltpu.SMEM((count,), jnp.int32),
            pltpu.SMEM((count,), jnp.int32),
            pltpu.VMEM((half, pixels, chans), BF16),
            pltpu.SemaphoreType.DMA((SPREAD + 1,)),
            pltpu.SemaphoreType.DMA,
        ],
        compiler_params=params(60),
        cost_estimate=cost(0, 10 * half * pixels * chans),
        name="spread",
    )(frame_time, cot)


def side_by_side(block, width):
    rows, chans = block.shape
    wide = block.astype(F32)
    col = lax.broadcasted_iota(jnp.int32, (rows, chans), 0) & (width - 1)
    left = jnp.where(col == 0, 0.0, pltpu.roll(wide, 1, 0)).astype(BF16)
    right = jnp.where(col == width - 1, 0.0, pltpu.roll(wide, rows - 1, 0)).astype(BF16)
    return left, block, right


def store_cat(cat, start, block, width):
    rows, chans = block.shape
    for j, part in enumerate(side_by_side(block, width)):
        cat[pl.ds(start, rows), j * chans : (j + 1) * chans] = part


def forward_kernel(width, x, w, acts, slope, cat):
    step = pl.program_id(0)
    pixels, chans = x.shape
    rows = acts.shape[0]

    @pl.when(step == 0)
    def _():
        cat[0:width] = jnp.zeros((width, 3 * chans), BF16)
        cat[width + pixels :] = jnp.zeros((width, 3 * chans), BF16)

        def fill(k, carry):
            at = pl.multiple_of(k * rows, rows)
            store_cat(cat, width + at, x[pl.ds(at, rows)], width)
            return carry

        lax.fori_loop(0, pixels // rows, fill, 0)

    at = pl.multiple_of(step * rows, rows)
    hidden = dot(cat[pl.ds(at, rows)], w[0])
    hidden = hidden + dot(cat[pl.ds(at + width, rows)], w[1])
    hidden = hidden + dot(cat[pl.ds(at + 2 * width, rows)], w[2])
    sig = 1.0 / (1.0 + jnp.exp(-hidden))
    acts[...] = (hidden * sig).astype(BF16)
    slope[...] = sig * (1.0 + hidden * (1.0 - sig))


def forward_call(x, w, width, steps=4):
    pixels, chans = x.shape
    rows = pixels // steps
    whole = lambda shape: pl.BlockSpec(shape, lambda k: (0,) * len(shape))
    tile = pl.BlockSpec((rows, chans), lambda k: (k, 0))
    return pl.pallas_call(
        functools.partial(forward_kernel, width),
        grid=(steps,),
        out_shape=(jax.ShapeDtypeStruct((pixels, chans), BF16), jax.ShapeDtypeStruct((pixels, chans), F32)),
        in_specs=[whole(x.shape), whole(w.shape)],
        out_specs=(tile, tile),
        scratch_shapes=[pltpu.VMEM((pixels + 2 * width, 3 * chans), BF16)],
        compiler_params=params(),
        cost_estimate=cost(18 * pixels * chans * chans, 8 * pixels * chans, 2 * pixels * chans),
        name="spatial_forward",
    )(x, w)


def filter_kernel(
    width, cuts, place, recv, slope_in, acts_in, frames_in, padded_in, w_time_in, hidden_grad, keep, send,
    w_time_t, lead, trail, slope, acts_t, frames_t, padded_t, hidden, ws, wt, arrived, left
):
    pixels, chans = slope.shape
    tile_pixels = recv.shape[2]
    edge = 2 * width

    def fetch(k):
        start, stop = cuts[k], cuts[k + 1]
        at = pl.ds(start, stop - start)
        those = pl.ds(start // tile_pixels, (stop - start) // tile_pixels)
        late = start + edge if k else 0
        beyond = pl.ds(late, stop + edge - late)
        pairs = (
            (recv.at[those, 0], lead.at[those]),
            (recv.at[those, 1], trail.at[those]),
            (slope_in.at[at], slope.at[at]),
            (acts_in.at[:, at], acts_t.at[:, at]),
            (frames_in.at[:, at], frames_t.at[:, at]),
            (padded_in.at[:, beyond], padded_t.at[:, beyond]),
        )
        return [pltpu.make_async_copy(a, b, arrived.at[k, n]) for n, (a, b) in enumerate(pairs)]

    copies = [fetch(k) for k in range(len(cuts) - 1)]
    copies[0].append(pltpu.make_async_copy(w_time_in, w_time_t, arrived.at[0, 6]))
    for copy in copies[0]:
        copy.start()

    time, core, count = place[0], place[1], place[2]
    even = lax.rem(time, 2) == 0
    has_trail = jnp.where(even, time == 0, time < count - 1)
    trail_weight = jnp.where(has_trail, 1.0, 0.0)

    share = chans // 4

    def put(tap, block):
        turned = block.T
        for half in range(2):
            at = (half * 12 + tap) * share
            one = turned[2 * half * share : (2 * half + 1) * share]
            two = turned[(2 * half + 1) * share : (2 * half + 2) * share]
            keep[at : at + share] = jnp.where(core == 0, one, two)
            send[at : at + share] = jnp.where(core == 0, two, one).astype(BF16)

    def add(total, rows, at, k, term):
        rows = slice(rows * chans, (rows + 1) * chans)
        term = total[rows, at] + term if k else term
        if k + 2 < len(cuts):
            total[rows, at] = term
        return term

    leaving = []
    for k, start in enumerate(cuts[:-1]):
        stop = cuts[k + 1]
        at, those = slice(start, stop), slice(start // tile_pixels, stop // tile_pixels)
        for copy in copies[k]:
            copy.wait()
        if k == 0:
            w_lead = w_time_t[jnp.where(even, 1, 2)]
            w_trail = (w_time_t[0].astype(F32) * trail_weight).astype(BF16)
        for copy in copies[k + 1] if k + 2 < len(cuts) else ():
            copy.start()
        lead_tile = lead[those].reshape(stop - start, chans)
        trail_tile = trail[those].reshape(stop - start, chans)
        grad = (dot(lead_tile, w_lead) + dot(trail_tile, w_trail)).astype(BF16)
        block = (grad.astype(F32) * slope[at]).astype(BF16)
        hidden[at] = block
        span = pl.ds(start, stop - start)
        leaving.append(pltpu.make_async_copy(hidden.at[span], hidden_grad.at[span], left.at[k]))
        leaving[-1].start()
        last = k + 2 == len(cuts)
        trail_term = add(wt, 0, slice(0, chans), k, dot(acts_t[:, at], trail_tile))
        lead_term = add(wt, 0, slice(chans, 2 * chans), k, dot(acts_t[:, at], lead_tile))
        right = jnp.concatenate(side_by_side(block, width)[::-1], axis=1)
        above, below = padded_t[:, at], padded_t[:, start + edge : stop + edge]
        if last:
            put(9, trail_term * trail_weight)
            put(10, lead_term * jnp.where(even, 1.0, 0.0))
            put(11, lead_term * jnp.where(even, 0.0, 1.0))
        for i, rows in enumerate((above, frames_t[:, at], below)):
            term = add(ws, i, slice(None), k, dot(rows, right))
            for j in range(3) if last else ():
                put(3 * i + j, term[:, j * chans : (j + 1) * chans])
    for copy in leaving:
        copy.wait()


def filter_call(place, recv, slope, acts_t, frames_t, padded_t, w_time_t, width, pieces=(1, 1, 1, 1)):
    pixels, chans = slope.shape
    count, _, tile_pixels, _ = recv.shape
    half = (6 * chans, chans)
    cuts = [pixels * sum(pieces[:k]) // sum(pieces) for k in range(len(pieces) + 1)]
    return pl.pallas_call(
        functools.partial(filter_kernel, width, cuts),
        out_shape=(
            pltpu.HBM((pixels, chans), BF16),
            pltpu.VMEM(half, F32),
            pltpu.VMEM(half, BF16),
        ),
        in_specs=[smem()] + [hbm()] * 6,
        out_specs=(hbm(), vmem(), vmem()),
        scratch_shapes=[
            pltpu.VMEM(w_time_t.shape, BF16),
            pltpu.VMEM((count, tile_pixels, chans), BF16),
            pltpu.VMEM((count, tile_pixels, chans), BF16),
            pltpu.VMEM((pixels, chans), F32),
            pltpu.VMEM((chans, pixels), BF16),
            pltpu.VMEM((chans, pixels), BF16),
            pltpu.VMEM((chans, pixels + 2 * width), BF16),
            pltpu.VMEM((pixels, chans), BF16),
            pltpu.VMEM((3 * chans, 3 * chans), F32),
            pltpu.VMEM((chans, 2 * chans), F32),
            pltpu.SemaphoreType.DMA((len(pieces), 7)),
            pltpu.SemaphoreType.DMA((len(pieces),)),
        ],
        compiler_params=params(40),
        cost_estimate=cost(26 * pixels * chans * chans, 18 * pixels * chans),
        name="filters",
    )(place, *(far(x) for x in (recv, slope, acts_t, frames_t, padded_t, w_time_t)))


def back_kernel(width, hidden_grad, w, out, cat):
    step = pl.program_id(0)
    pixels, chans = hidden_grad.shape
    rows = out.shape[0]

    @pl.when(step == 0)
    def _():
        cat[0:width] = jnp.zeros((width, 3 * chans), BF16)
        cat[width + pixels :] = jnp.zeros((width, 3 * chans), BF16)

        def fill(k, carry):
            at = pl.multiple_of(k * rows, rows)
            store_cat(cat, width + at, hidden_grad[pl.ds(at, rows)], width)
            return carry

        lax.fori_loop(0, pixels // rows, fill, 0)

    at = pl.multiple_of(step * rows, rows)
    total = dot(cat[pl.ds(at, rows)], w[0])
    total = total + dot(cat[pl.ds(at + width, rows)], w[1])
    total = total + dot(cat[pl.ds(at + 2 * width, rows)], w[2])
    out[...] = total.astype(BF16)


def back_call(hidden_grad, w, width, steps=4):
    pixels, chans = hidden_grad.shape
    rows = pixels // steps
    whole = lambda shape: pl.BlockSpec(shape, lambda k: (0,) * len(shape))
    return pl.pallas_call(
        functools.partial(back_kernel, width),
        grid=(steps,),
        out_shape=jax.ShapeDtypeStruct((pixels, chans), BF16),
        in_specs=[whole(hidden_grad.shape), whole(w.shape)],
        out_specs=pl.BlockSpec((rows, chans), lambda k: (k, 0)),
        scratch_shapes=[pltpu.VMEM((pixels + 2 * width, 3 * chans), BF16)],
        compiler_params=params(),
        cost_estimate=cost(18 * pixels * chans * chans, 4 * pixels * chans),
        name="spatial_back",
    )(hidden_grad, w)


def total_kernel(factor, parts, out):
    def add(k, total):
        return total + parts[k].astype(F32)

    total = lax.fori_loop(1, parts.shape[0], add, parts[0].astype(F32), unroll=True)
    mine = (total * factor).astype(BF16)
    for k in range(out.shape[0]):
        out[k] = mine


def total_call(parts, factor, copies):
    sources, depth, chans = parts.shape
    return pl.pallas_call(
        functools.partial(total_kernel, factor),
        out_shape=jax.ShapeDtypeStruct((copies, depth, chans), BF16),
        in_specs=[vmem()],
        out_specs=vmem(),
        compiler_params=params(),
        cost_estimate=cost(sources * depth * chans, 3 * sources * depth * chans),
        name="total",
    )(parts)


def turn_kernel(rows, ws, wt):
    taps = ws.shape[0] + wt.shape[0]
    share = rows.shape[0] // taps
    for tap in range(taps):
        block = rows[tap * share : (tap + 1) * share].astype(F32)
        if tap < ws.shape[0]:
            ws[tap] = block
        else:
            wt[tap - ws.shape[0]] = block


def turn_call(rows, share):
    chans = rows.shape[1]
    return pl.pallas_call(
        turn_kernel,
        out_shape=(jax.ShapeDtypeStruct((9, share, chans), F32), jax.ShapeDtypeStruct((3, share, chans), F32)),
        in_specs=[vmem()],
        out_specs=(vmem(), vmem()),
        compiler_params=params(),
        cost_estimate=cost(0, 6 * rows.shape[0] * chans),
        name="turn",
    )(rows)


def exchange(x, axes):
    return lax.all_to_all(x, axes, split_axis=0, concat_axis=0, tiled=True)


def local(clip_frames, w_spatial, w_time, cotangent, frame_time):
    count = frame_time.shape[0]
    height, width, chans = clip_frames.shape[2:]
    pixels = height * width
    clips = lax.axis_size("clip")
    groups = lax.axis_size("half") * lax.axis_size("core")
    share = chans // groups
    x = clip_frames.reshape(pixels, chans)

    recv = exchange(spread_call(frame_time, cotangent.reshape(count // 2, -1, chans)), "clip")
    acts, slope = forward_call(x, w_spatial.reshape(3, 3 * chans, chans), width)
    padded_t = jnp.pad(x.T, ((0, 0), (width, width)))
    place = jnp.stack([frame_time[lax.axis_index("clip")], lax.axis_index("core"), jnp.int32(count)])
    hidden_grad, keep, send = filter_call(
        place, recv, slope, acts.T, x.T, padded_t, w_time.transpose(0, 2, 1), width
    )
    w_back = w_spatial[::-1, ::-1].transpose(0, 1, 3, 2).reshape(3, 3 * chans, chans)
    clip_grad = back_call(hidden_grad, w_back, width)

    came = lax.ppermute(send, "core", [(0, 1), (1, 0)])
    depth = keep.shape[0] // (2 * clips)
    parts = (keep + came.astype(F32)).astype(BF16).reshape(2 * clips, depth, chans)
    parts = exchange(parts, ("half", "clip"))
    parts, clip_grad = lax.optimization_barrier((parts, clip_grad))
    factor = 1.0 / math.sqrt(clip_frames.shape[0] * groups * count * pixels)
    rows = exchange(total_call(parts, factor, clips), "clip")
    ws, wt = turn_call(rows.reshape(clips * depth, chans), share)
    ws = ws.reshape(3, 3, share, chans).transpose(0, 1, 3, 2)
    return (clip_grad.reshape(clip_frames.shape), ws, wt.transpose(0, 2, 1))


def solution(mesh):
    clips, groups = mesh.devices.shape
    parts = Mesh(mesh.devices.reshape(clips, 2, groups // 2), ("clip", "half", "core"))
    group = ("half", "core")
    return jax.shard_map(
        local,
        mesh=parts,
        in_specs=(
            P(group, "clip", None, None, None),
            P(),
            P(),
            P(group, None, "clip", None, None),
            P(),
        ),
        out_specs=(
            P(group, "clip", None, None, None),
            P(None, None, None, group),
            P(None, None, group),
        ),
        check_vma=False,
    )
```

```python
import functools
import math

import jax
import jax.numpy as jnp
from jax import lax
from jax.experimental import pallas as pl
from jax.experimental.pallas import tpu as pltpu
from jax.sharding import Mesh
from jax.sharding import PartitionSpec as P

SPREAD = 4
BF16 = jnp.bfloat16
F32 = jnp.float32


def dot(a, b, dims=((1,), (0,))):
    return lax.dot_general(a, b, (dims, ((), ())), preferred_element_type=F32)


def params(mib=24):
    return pltpu.CompilerParams(vmem_limit_bytes=mib * 1024 * 1024)


def vmem():
    return pl.BlockSpec(memory_space=pltpu.VMEM)


def hbm():
    return pl.BlockSpec(memory_space=pltpu.HBM)


def smem():
    return pl.BlockSpec(memory_space=pltpu.SMEM)


def far(x):
    return pltpu.with_memory_space_constraint(x, pltpu.HBM)


def cost(flops, nbytes, trans=0):
    return pl.CostEstimate(flops=flops, bytes_accessed=nbytes, transcendentals=trans)


def spread_kernel(times, cot, out, frame_time, place, held, load, sent):
    half = held.shape[0]
    count = out.shape[0]
    order = pltpu.make_async_copy(times, frame_time, load.at[0])
    order.start()
    span = half // (load.shape[0] - 1)
    pieces = []
    for k in range(load.shape[0] - 1):
        at = pl.ds(k * span, span)
        pieces.append(pltpu.make_async_copy(cot.at[at], held.at[at], load.at[k + 1]))
        pieces[-1].start()
    order.wait()

    def put(s, carry):
        place[frame_time[s]] = s
        return carry

    lax.fori_loop(0, count, put, 0)
    for k, piece in enumerate(pieces):
        piece.wait()
        for u in range(k * span, (k + 1) * span):
            leads = (2 * u, 2 * u + 1)
            trails = tuple(t for t in range(count) if min((t + 1) // 2, half - 1) == u)
            for which, wanted in enumerate((leads, trails)):
                for t in wanted:
                    pltpu.make_async_copy(held.at[u], out.at[place[t], which], sent).start()
    pltpu.make_async_copy(out, out, sent).wait()


def spread_call(frame_time, cot):
    half, pixels, chans = cot.shape
    count = frame_time.shape[0]
    return pl.pallas_call(
        spread_kernel,
        out_shape=jax.ShapeDtypeStruct((count, 2, pixels, chans), BF16),
        in_specs=[hbm(), hbm()],
        out_specs=hbm(),
        scratch_shapes=[
            pltpu.SMEM((count,), jnp.int32),
            pltpu.SMEM((count,), jnp.int32),
            pltpu.VMEM((half, pixels, chans), BF16),
            pltpu.SemaphoreType.DMA((SPREAD + 1,)),
            pltpu.SemaphoreType.DMA,
        ],
        compiler_params=params(60),
        cost_estimate=cost(0, 10 * half * pixels * chans),
        name="spread",
    )(frame_time, cot)


def side_by_side(block, width):
    rows, chans = block.shape
    wide = block.astype(F32)
    col = lax.broadcasted_iota(jnp.int32, (rows, chans), 0) & (width - 1)
    left = jnp.where(col == 0, 0.0, pltpu.roll(wide, 1, 0)).astype(BF16)
    right = jnp.where(col == width - 1, 0.0, pltpu.roll(wide, rows - 1, 0)).astype(BF16)
    return left, block, right


def store_cat(cat, start, block, width):
    rows, chans = block.shape
    for j, part in enumerate(side_by_side(block, width)):
        cat[pl.ds(start, rows), j * chans : (j + 1) * chans] = part


def forward_kernel(width, x, w, acts, slope, cat):
    step = pl.program_id(0)
    pixels, chans = x.shape
    rows = acts.shape[0]

    @pl.when(step == 0)
    def _():
        cat[0:width] = jnp.zeros((width, 3 * chans), BF16)
        cat[width + pixels :] = jnp.zeros((width, 3 * chans), BF16)

        def fill(k, carry):
            at = pl.multiple_of(k * rows, rows)
            store_cat(cat, width + at, x[pl.ds(at, rows)], width)
            return carry

        lax.fori_loop(0, pixels // rows, fill, 0)

    at = pl.multiple_of(step * rows, rows)
    hidden = dot(cat[pl.ds(at, rows)], w[0])
    hidden = hidden + dot(cat[pl.ds(at + width, rows)], w[1])
    hidden = hidden + dot(cat[pl.ds(at + 2 * width, rows)], w[2])
    sig = 1.0 / (1.0 + jnp.exp(-hidden))
    acts[...] = (hidden * sig).astype(BF16)
    slope[...] = sig * (1.0 + hidden * (1.0 - sig))


def forward_call(x, w, width, steps=4):
    pixels, chans = x.shape
    rows = pixels // steps
    whole = lambda shape: pl.BlockSpec(shape, lambda k: (0,) * len(shape))
    tile = pl.BlockSpec((rows, chans), lambda k: (k, 0))
    return pl.pallas_call(
        functools.partial(forward_kernel, width),
        grid=(steps,),
        out_shape=(jax.ShapeDtypeStruct((pixels, chans), BF16), jax.ShapeDtypeStruct((pixels, chans), F32)),
        in_specs=[whole(x.shape), whole(w.shape)],
        out_specs=(tile, tile),
        scratch_shapes=[pltpu.VMEM((pixels + 2 * width, 3 * chans), BF16)],
        compiler_params=params(),
        cost_estimate=cost(18 * pixels * chans * chans, 8 * pixels * chans, 2 * pixels * chans),
        name="spatial_forward",
    )(x, w)


def filter_kernel(
    width, cuts, place, recv, slope_in, acts_in, frames_in, padded_in, w_time_in, hidden_grad, keep, send,
    w_time_t, lead, trail, slope, acts_t, frames_t, padded_t, hidden, ws, wt, arrived, left
):
    pixels, chans = slope.shape
    tile_pixels = recv.shape[2]
    edge = 2 * width

    def fetch(k):
        start, stop = cuts[k], cuts[k + 1]
        at = pl.ds(start, stop - start)
        those = pl.ds(start // tile_pixels, (stop - start) // tile_pixels)
        late = start + edge if k else 0
        beyond = pl.ds(late, stop + edge - late)
        pairs = (
            (recv.at[those, 0], lead.at[those]),
            (recv.at[those, 1], trail.at[those]),
            (slope_in.at[at], slope.at[at]),
            (acts_in.at[:, at], acts_t.at[:, at]),
            (frames_in.at[:, at], frames_t.at[:, at]),
            (padded_in.at[:, beyond], padded_t.at[:, beyond]),
        )
        return [pltpu.make_async_copy(a, b, arrived.at[k, n]) for n, (a, b) in enumerate(pairs)]

    copies = [fetch(k) for k in range(len(cuts) - 1)]
    copies[0].append(pltpu.make_async_copy(w_time_in, w_time_t, arrived.at[0, 6]))
    for copy in copies[0]:
        copy.start()

    time, core, count = place[0], place[1], place[2]
    even = lax.rem(time, 2) == 0
    has_trail = jnp.where(even, time == 0, time < count - 1)
    trail_weight = jnp.where(has_trail, 1.0, 0.0)

    share = chans // 4

    def put(tap, block):
        turned = block.T
        for half in range(2):
            at = (half * 12 + tap) * share
            one = turned[2 * half * share : (2 * half + 1) * share]
            two = turned[(2 * half + 1) * share : (2 * half + 2) * share]
            keep[at : at + share] = jnp.where(core == 0, one, two)
            send[at : at + share] = jnp.where(core == 0, two, one).astype(BF16)

    def add(total, rows, at, k, term):
        rows = slice(rows * chans, (rows + 1) * chans)
        term = total[rows, at] + term if k else term
        if k + 2 < len(cuts):
            total[rows, at] = term
        return term

    leaving = []
    for k, start in enumerate(cuts[:-1]):
        stop = cuts[k + 1]
        at, those = slice(start, stop), slice(start // tile_pixels, stop // tile_pixels)
        for copy in copies[k]:
            copy.wait()
        if k == 0:
            w_lead = w_time_t[jnp.where(even, 1, 2)]
            w_trail = (w_time_t[0].astype(F32) * trail_weight).astype(BF16)
        for copy in copies[k + 1] if k + 2 < len(cuts) else ():
            copy.start()
        for copy in leaving[-1:]:
            copy.start()
        lead_tile = lead[those].reshape(stop - start, chans)
        trail_tile = trail[those].reshape(stop - start, chans)
        grad = (dot(lead_tile, w_lead) + dot(trail_tile, w_trail)).astype(BF16)
        block = (grad.astype(F32) * slope[at]).astype(BF16)
        hidden[at] = block
        span = pl.ds(start, stop - start)
        leaving.append(pltpu.make_async_copy(hidden.at[span], hidden_grad.at[span], left.at[k]))
        last = k + 2 == len(cuts)
        trail_term = add(wt, 0, slice(0, chans), k, dot(acts_t[:, at], trail_tile))
        lead_term = add(wt, 0, slice(chans, 2 * chans), k, dot(acts_t[:, at], lead_tile))
        right = jnp.concatenate(side_by_side(block, width)[::-1], axis=1)
        above, below = padded_t[:, at], padded_t[:, start + edge : stop + edge]
        if last:
            put(9, trail_term * trail_weight)
            put(10, lead_term * jnp.where(even, 1.0, 0.0))
            put(11, lead_term * jnp.where(even, 0.0, 1.0))
        for i, rows in enumerate((above, frames_t[:, at], below)):
            term = add(ws, i, slice(None), k, dot(rows, right))
            for j in range(3) if last else ():
                put(3 * i + j, term[:, j * chans : (j + 1) * chans])
    leaving[-1].start()
    for copy in leaving:
        copy.wait()


def filter_call(place, recv, slope, acts_t, frames_t, padded_t, w_time_t, width, pieces=(1, 1, 1, 1)):
    pixels, chans = slope.shape
    count, _, tile_pixels, _ = recv.shape
    half = (6 * chans, chans)
    cuts = [pixels * sum(pieces[:k]) // sum(pieces) for k in range(len(pieces) + 1)]
    return pl.pallas_call(
        functools.partial(filter_kernel, width, cuts),
        out_shape=(
            pltpu.HBM((pixels, chans), BF16),
            pltpu.VMEM(half, F32),
            pltpu.VMEM(half, BF16),
        ),
        in_specs=[smem()] + [hbm()] * 6,
        out_specs=(hbm(), vmem(), vmem()),
        scratch_shapes=[
            pltpu.VMEM(w_time_t.shape, BF16),
            pltpu.VMEM((count, tile_pixels, chans), BF16),
            pltpu.VMEM((count, tile_pixels, chans), BF16),
            pltpu.VMEM((pixels, chans), F32),
            pltpu.VMEM((chans, pixels), BF16),
            pltpu.VMEM((chans, pixels), BF16),
            pltpu.VMEM((chans, pixels + 2 * width), BF16),
            pltpu.VMEM((pixels, chans), BF16),
            pltpu.VMEM((3 * chans, 3 * chans), F32),
            pltpu.VMEM((chans, 2 * chans), F32),
            pltpu.SemaphoreType.DMA((len(pieces), 7)),
            pltpu.SemaphoreType.DMA((len(pieces),)),
        ],
        compiler_params=params(40),
        cost_estimate=cost(26 * pixels * chans * chans, 18 * pixels * chans),
        name="filters",
    )(place, *(far(x) for x in (recv, slope, acts_t, frames_t, padded_t, w_time_t)))


def back_kernel(width, hidden_grad, w, out, cat):
    step = pl.program_id(0)
    pixels, chans = hidden_grad.shape
    rows = out.shape[0]

    @pl.when(step == 0)
    def _():
        cat[0:width] = jnp.zeros((width, 3 * chans), BF16)
        cat[width + pixels :] = jnp.zeros((width, 3 * chans), BF16)

        def fill(k, carry):
            at = pl.multiple_of(k * rows, rows)
            store_cat(cat, width + at, hidden_grad[pl.ds(at, rows)], width)
            return carry

        lax.fori_loop(0, pixels // rows, fill, 0)

    at = pl.multiple_of(step * rows, rows)
    total = dot(cat[pl.ds(at, rows)], w[0])
    total = total + dot(cat[pl.ds(at + width, rows)], w[1])
    total = total + dot(cat[pl.ds(at + 2 * width, rows)], w[2])
    out[...] = total.astype(BF16)


def back_call(hidden_grad, w, width, steps=4):
    pixels, chans = hidden_grad.shape
    rows = pixels // steps
    whole = lambda shape: pl.BlockSpec(shape, lambda k: (0,) * len(shape))
    return pl.pallas_call(
        functools.partial(back_kernel, width),
        grid=(steps,),
        out_shape=jax.ShapeDtypeStruct((pixels, chans), BF16),
        in_specs=[whole(hidden_grad.shape), whole(w.shape)],
        out_specs=pl.BlockSpec((rows, chans), lambda k: (k, 0)),
        scratch_shapes=[pltpu.VMEM((pixels + 2 * width, 3 * chans), BF16)],
        compiler_params=params(),
        cost_estimate=cost(18 * pixels * chans * chans, 4 * pixels * chans),
        name="spatial_back",
    )(hidden_grad, w)


def total_kernel(factor, parts, out):
    def add(k, total):
        return total + parts[k].astype(F32)

    total = lax.fori_loop(1, parts.shape[0], add, parts[0].astype(F32), unroll=True)
    mine = (total * factor).astype(BF16)
    for k in range(out.shape[0]):
        out[k] = mine


def total_call(parts, factor, copies):
    sources, depth, chans = parts.shape
    return pl.pallas_call(
        functools.partial(total_kernel, factor),
        out_shape=jax.ShapeDtypeStruct((copies, depth, chans), BF16),
        in_specs=[vmem()],
        out_specs=vmem(),
        compiler_params=params(),
        cost_estimate=cost(sources * depth * chans, 3 * sources * depth * chans),
        name="total",
    )(parts)


def turn_kernel(rows, ws, wt):
    taps = ws.shape[0] + wt.shape[0]
    share = rows.shape[0] // taps
    for tap in range(taps):
        block = rows[tap * share : (tap + 1) * share].astype(F32)
        if tap < ws.shape[0]:
            ws[tap] = block
        else:
            wt[tap - ws.shape[0]] = block


def turn_call(rows, share):
    chans = rows.shape[1]
    return pl.pallas_call(
        turn_kernel,
        out_shape=(jax.ShapeDtypeStruct((9, share, chans), F32), jax.ShapeDtypeStruct((3, share, chans), F32)),
        in_specs=[vmem()],
        out_specs=(vmem(), vmem()),
        compiler_params=params(),
        cost_estimate=cost(0, 6 * rows.shape[0] * chans),
        name="turn",
    )(rows)


def exchange(x, axes):
    return lax.all_to_all(x, axes, split_axis=0, concat_axis=0, tiled=True)


def local(clip_frames, w_spatial, w_time, cotangent, frame_time):
    count = frame_time.shape[0]
    height, width, chans = clip_frames.shape[2:]
    pixels = height * width
    clips = lax.axis_size("clip")
    groups = lax.axis_size("half") * lax.axis_size("core")
    share = chans // groups
    x = clip_frames.reshape(pixels, chans)

    recv = exchange(spread_call(frame_time, cotangent.reshape(count // 2, -1, chans)), "clip")
    acts, slope = forward_call(x, w_spatial.reshape(3, 3 * chans, chans), width)
    padded_t = jnp.pad(x.T, ((0, 0), (width, width)))
    place = jnp.stack([frame_time[lax.axis_index("clip")], lax.axis_index("core"), jnp.int32(count)])
    hidden_grad, keep, send = filter_call(
        place, recv, slope, acts.T, x.T, padded_t, w_time.transpose(0, 2, 1), width
    )
    w_back = w_spatial[::-1, ::-1].transpose(0, 1, 3, 2).reshape(3, 3 * chans, chans)
    clip_grad = back_call(hidden_grad, w_back, width)

    came = lax.ppermute(send, "core", [(0, 1), (1, 0)])
    depth = keep.shape[0] // (2 * clips)
    parts = (keep + came.astype(F32)).astype(BF16).reshape(2 * clips, depth, chans)
    parts = exchange(parts, ("half", "clip"))
    parts, clip_grad = lax.optimization_barrier((parts, clip_grad))
    factor = 1.0 / math.sqrt(clip_frames.shape[0] * groups * count * pixels)
    rows = exchange(total_call(parts, factor, clips), "clip")
    ws, wt = turn_call(rows.reshape(clips * depth, chans), share)
    ws = ws.reshape(3, 3, share, chans).transpose(0, 1, 3, 2)
    return (clip_grad.reshape(clip_frames.shape), ws, wt.transpose(0, 2, 1))


def solution(mesh):
    clips, groups = mesh.devices.shape
    parts = Mesh(mesh.devices.reshape(clips, 2, groups // 2), ("clip", "half", "core"))
    group = ("half", "core")
    return jax.shard_map(
        local,
        mesh=parts,
        in_specs=(
            P(group, "clip", None, None, None),
            P(),
            P(),
            P(group, None, "clip", None, None),
            P(),
        ),
        out_specs=(
            P(group, "clip", None, None, None),
            P(None, None, None, group),
            P(None, None, group),
        ),
        check_vma=False,
    )
```

```python
import functools
import math

import jax
import jax.numpy as jnp
from jax import lax
from jax.experimental import pallas as pl
from jax.experimental.pallas import tpu as pltpu
from jax.sharding import Mesh
from jax.sharding import PartitionSpec as P

SPREAD = 4
BF16 = jnp.bfloat16
F32 = jnp.float32


def dot(a, b, dims=((1,), (0,))):
    return lax.dot_general(a, b, (dims, ((), ())), preferred_element_type=F32)


def params(mib=24):
    return pltpu.CompilerParams(vmem_limit_bytes=mib * 1024 * 1024)


def vmem():
    return pl.BlockSpec(memory_space=pltpu.VMEM)


def hbm():
    return pl.BlockSpec(memory_space=pltpu.HBM)


def smem():
    return pl.BlockSpec(memory_space=pltpu.SMEM)


def far(x):
    return pltpu.with_memory_space_constraint(x, pltpu.HBM)


def cost(flops, nbytes, trans=0):
    return pl.CostEstimate(flops=flops, bytes_accessed=nbytes, transcendentals=trans)


def spread_kernel(times, cot, out, frame_time, place, held, load, sent):
    half = held.shape[0]
    count = out.shape[0]
    order = pltpu.make_async_copy(times, frame_time, load.at[0])
    order.start()
    span = half // (load.shape[0] - 1)
    pieces = []
    for k in range(load.shape[0] - 1):
        at = pl.ds(k * span, span)
        pieces.append(pltpu.make_async_copy(cot.at[at], held.at[at], load.at[k + 1]))
        pieces[-1].start()
    order.wait()

    def put(s, carry):
        place[frame_time[s]] = s
        return carry

    lax.fori_loop(0, count, put, 0)
    for k, piece in enumerate(pieces):
        piece.wait()
        for u in range(k * span, (k + 1) * span):
            leads = (2 * u, 2 * u + 1)
            trails = tuple(t for t in range(count) if min((t + 1) // 2, half - 1) == u)
            for which, wanted in enumerate((leads, trails)):
                for t in wanted:
                    pltpu.make_async_copy(held.at[u], out.at[place[t], which], sent).start()
    pltpu.make_async_copy(out, out, sent).wait()


def spread_call(frame_time, cot):
    half, pixels, chans = cot.shape
    count = frame_time.shape[0]
    return pl.pallas_call(
        spread_kernel,
        out_shape=jax.ShapeDtypeStruct((count, 2, pixels, chans), BF16),
        in_specs=[hbm(), hbm()],
        out_specs=hbm(),
        scratch_shapes=[
            pltpu.SMEM((count,), jnp.int32),
            pltpu.SMEM((count,), jnp.int32),
            pltpu.VMEM((half, pixels, chans), BF16),
            pltpu.SemaphoreType.DMA((SPREAD + 1,)),
            pltpu.SemaphoreType.DMA,
        ],
        compiler_params=params(60),
        cost_estimate=cost(0, 10 * half * pixels * chans),
        name="spread",
    )(frame_time, cot)


def side_by_side(block, width):
    rows, chans = block.shape
    col = lax.broadcasted_iota(jnp.int32, (rows, chans), 0) & (width - 1)
    none = jnp.zeros((), BF16)
    left = jnp.where(col == 0, none, pltpu.roll(block, 1, 0))
    right = jnp.where(col == width - 1, none, pltpu.roll(block, rows - 1, 0))
    return left, block, right


def store_cat(cat, start, block, width):
    rows, chans = block.shape
    for j, part in enumerate(side_by_side(block, width)):
        cat[pl.ds(start, rows), j * chans : (j + 1) * chans] = part


def forward_kernel(width, x, w, acts, slope, cat):
    step = pl.program_id(0)
    pixels, chans = x.shape
    rows = acts.shape[0]

    @pl.when(step == 0)
    def _():
        cat[0:width] = jnp.zeros((width, 3 * chans), BF16)
        cat[width + pixels :] = jnp.zeros((width, 3 * chans), BF16)

        def fill(k, carry):
            at = pl.multiple_of(k * rows, rows)
            store_cat(cat, width + at, x[pl.ds(at, rows)], width)
            return carry

        lax.fori_loop(0, pixels // rows, fill, 0)

    at = pl.multiple_of(step * rows, rows)
    hidden = dot(cat[pl.ds(at, rows)], w[0])
    hidden = hidden + dot(cat[pl.ds(at + width, rows)], w[1])
    hidden = hidden + dot(cat[pl.ds(at + 2 * width, rows)], w[2])
    sig = 1.0 / (1.0 + jnp.exp(-hidden))
    acts[...] = (hidden * sig).astype(BF16)
    slope[...] = sig * (1.0 + hidden * (1.0 - sig))


def forward_call(x, w, width, steps=4):
    pixels, chans = x.shape
    rows = pixels // steps
    whole = lambda shape: pl.BlockSpec(shape, lambda k: (0,) * len(shape))
    tile = pl.BlockSpec((rows, chans), lambda k: (k, 0))
    return pl.pallas_call(
        functools.partial(forward_kernel, width),
        grid=(steps,),
        out_shape=(jax.ShapeDtypeStruct((pixels, chans), BF16), jax.ShapeDtypeStruct((pixels, chans), F32)),
        in_specs=[whole(x.shape), whole(w.shape)],
        out_specs=(tile, tile),
        scratch_shapes=[pltpu.VMEM((pixels + 2 * width, 3 * chans), BF16)],
        compiler_params=params(),
        cost_estimate=cost(18 * pixels * chans * chans, 8 * pixels * chans, 2 * pixels * chans),
        name="spatial_forward",
    )(x, w)


def filter_kernel(
    width, cuts, place, recv, slope_in, acts_in, frames_in, padded_in, w_time_in, hidden_grad, keep, send,
    w_time_t, lead, trail, slope, acts_t, frames_t, padded_t, hidden, ws, wt, arrived, left
):
    pixels, chans = slope.shape
    tile_pixels = recv.shape[2]
    edge = 2 * width

    def fetch(k):
        start, stop = cuts[k], cuts[k + 1]
        at = pl.ds(start, stop - start)
        those = pl.ds(start // tile_pixels, (stop - start) // tile_pixels)
        late = start + edge if k else 0
        beyond = pl.ds(late, stop + edge - late)
        pairs = (
            (recv.at[those, 0], lead.at[those]),
            (recv.at[those, 1], trail.at[those]),
            (slope_in.at[at], slope.at[at]),
            (acts_in.at[:, at], acts_t.at[:, at]),
            (frames_in.at[:, at], frames_t.at[:, at]),
            (padded_in.at[:, beyond], padded_t.at[:, beyond]),
        )
        return [pltpu.make_async_copy(a, b, arrived.at[k, n]) for n, (a, b) in enumerate(pairs)]

    copies = [fetch(k) for k in range(len(cuts) - 1)]
    copies[0].append(pltpu.make_async_copy(w_time_in, w_time_t, arrived.at[0, 6]))
    for copy in copies[0]:
        copy.start()

    time, core, count = place[0], place[1], place[2]
    even = lax.rem(time, 2) == 0
    has_trail = jnp.where(even, time == 0, time < count - 1)
    trail_weight = jnp.where(has_trail, 1.0, 0.0)

    share = chans // 4

    def put(tap, block):
        turned = block.T
        for half in range(2):
            at = (half * 12 + tap) * share
            one = turned[2 * half * share : (2 * half + 1) * share]
            two = turned[(2 * half + 1) * share : (2 * half + 2) * share]
            keep[at : at + share] = jnp.where(core == 0, one, two)
            send[at : at + share] = jnp.where(core == 0, two, one).astype(BF16)

    def add(total, rows, at, k, term):
        rows = slice(rows * chans, (rows + 1) * chans)
        term = total[rows, at] + term if k else term
        if k + 2 < len(cuts):
            total[rows, at] = term
        return term

    leaving = []
    for k, start in enumerate(cuts[:-1]):
        stop = cuts[k + 1]
        at, those = slice(start, stop), slice(start // tile_pixels, stop // tile_pixels)
        for copy in copies[k]:
            copy.wait()
        if k == 0:
            w_lead = w_time_t[jnp.where(even, 1, 2)]
            w_trail = (w_time_t[0].astype(F32) * trail_weight).astype(BF16)
        for copy in copies[k + 1] if k + 2 < len(cuts) else ():
            copy.start()
        for copy in leaving[-1:]:
            copy.start()
        lead_tile = lead[those].reshape(stop - start, chans)
        trail_tile = trail[those].reshape(stop - start, chans)
        grad = (dot(lead_tile, w_lead) + dot(trail_tile, w_trail)).astype(BF16)
        block = (grad.astype(F32) * slope[at]).astype(BF16)
        hidden[at] = block
        span = pl.ds(start, stop - start)
        leaving.append(pltpu.make_async_copy(hidden.at[span], hidden_grad.at[span], left.at[k]))
        last = k + 2 == len(cuts)
        trail_term = add(wt, 0, slice(0, chans), k, dot(acts_t[:, at], trail_tile))
        lead_term = add(wt, 0, slice(chans, 2 * chans), k, dot(acts_t[:, at], lead_tile))
        right = jnp.concatenate(side_by_side(block, width)[::-1], axis=1)
        above, below = padded_t[:, at], padded_t[:, start + edge : stop + edge]
        if last:
            put(9, trail_term * trail_weight)
            put(10, lead_term * jnp.where(even, 1.0, 0.0))
            put(11, lead_term * jnp.where(even, 0.0, 1.0))
        for i, rows in enumerate((above, frames_t[:, at], below)):
            term = add(ws, i, slice(None), k, dot(rows, right))
            for j in range(3) if last else ():
                put(3 * i + j, term[:, j * chans : (j + 1) * chans])
    leaving[-1].start()
    for copy in leaving:
        copy.wait()


def filter_call(place, recv, slope, acts_t, frames_t, padded_t, w_time_t, width, pieces=(1, 1, 1, 1)):
    pixels, chans = slope.shape
    count, _, tile_pixels, _ = recv.shape
    half = (6 * chans, chans)
    cuts = [pixels * sum(pieces[:k]) // sum(pieces) for k in range(len(pieces) + 1)]
    return pl.pallas_call(
        functools.partial(filter_kernel, width, cuts),
        out_shape=(
            pltpu.HBM((pixels, chans), BF16),
            pltpu.VMEM(half, F32),
            pltpu.VMEM(half, BF16),
        ),
        in_specs=[smem()] + [hbm()] * 6,
        out_specs=(hbm(), vmem(), vmem()),
        scratch_shapes=[
            pltpu.VMEM(w_time_t.shape, BF16),
            pltpu.VMEM((count, tile_pixels, chans), BF16),
            pltpu.VMEM((count, tile_pixels, chans), BF16),
            pltpu.VMEM((pixels, chans), F32),
            pltpu.VMEM((chans, pixels), BF16),
            pltpu.VMEM((chans, pixels), BF16),
            pltpu.VMEM((chans, pixels + 2 * width), BF16),
            pltpu.VMEM((pixels, chans), BF16),
            pltpu.VMEM((3 * chans, 3 * chans), F32),
            pltpu.VMEM((chans, 2 * chans), F32),
            pltpu.SemaphoreType.DMA((len(pieces), 7)),
            pltpu.SemaphoreType.DMA((len(pieces),)),
        ],
        compiler_params=params(40),
        cost_estimate=cost(26 * pixels * chans * chans, 18 * pixels * chans),
        name="filters",
    )(place, *(far(x) for x in (recv, slope, acts_t, frames_t, padded_t, w_time_t)))


def back_kernel(width, hidden_grad, w, out, cat):
    step = pl.program_id(0)
    pixels, chans = hidden_grad.shape
    rows = out.shape[0]

    @pl.when(step == 0)
    def _():
        cat[0:width] = jnp.zeros((width, 3 * chans), BF16)
        cat[width + pixels :] = jnp.zeros((width, 3 * chans), BF16)

        def fill(k, carry):
            at = pl.multiple_of(k * rows, rows)
            store_cat(cat, width + at, hidden_grad[pl.ds(at, rows)], width)
            return carry

        lax.fori_loop(0, pixels // rows, fill, 0)

    at = pl.multiple_of(step * rows, rows)
    total = dot(cat[pl.ds(at, rows)], w[0])
    total = total + dot(cat[pl.ds(at + width, rows)], w[1])
    total = total + dot(cat[pl.ds(at + 2 * width, rows)], w[2])
    out[...] = total.astype(BF16)


def back_call(hidden_grad, w, width, steps=4):
    pixels, chans = hidden_grad.shape
    rows = pixels // steps
    whole = lambda shape: pl.BlockSpec(shape, lambda k: (0,) * len(shape))
    return pl.pallas_call(
        functools.partial(back_kernel, width),
        grid=(steps,),
        out_shape=jax.ShapeDtypeStruct((pixels, chans), BF16),
        in_specs=[whole(hidden_grad.shape), whole(w.shape)],
        out_specs=pl.BlockSpec((rows, chans), lambda k: (k, 0)),
        scratch_shapes=[pltpu.VMEM((pixels + 2 * width, 3 * chans), BF16)],
        compiler_params=params(),
        cost_estimate=cost(18 * pixels * chans * chans, 4 * pixels * chans),
        name="spatial_back",
    )(hidden_grad, w)


def total_kernel(factor, parts, out):
    def add(k, total):
        return total + parts[k].astype(F32)

    total = lax.fori_loop(1, parts.shape[0], add, parts[0].astype(F32), unroll=True)
    mine = (total * factor).astype(BF16)
    for k in range(out.shape[0]):
        out[k] = mine


def total_call(parts, factor, copies):
    sources, depth, chans = parts.shape
    return pl.pallas_call(
        functools.partial(total_kernel, factor),
        out_shape=jax.ShapeDtypeStruct((copies, depth, chans), BF16),
        in_specs=[vmem()],
        out_specs=vmem(),
        compiler_params=params(),
        cost_estimate=cost(sources * depth * chans, 3 * sources * depth * chans),
        name="total",
    )(parts)


def turn_kernel(rows, ws, wt):
    taps = ws.shape[0] + wt.shape[0]
    share = rows.shape[0] // taps
    for tap in range(taps):
        block = rows[tap * share : (tap + 1) * share].astype(F32)
        if tap < ws.shape[0]:
            ws[tap] = block
        else:
            wt[tap - ws.shape[0]] = block


def turn_call(rows, share):
    chans = rows.shape[1]
    return pl.pallas_call(
        turn_kernel,
        out_shape=(jax.ShapeDtypeStruct((9, share, chans), F32), jax.ShapeDtypeStruct((3, share, chans), F32)),
        in_specs=[vmem()],
        out_specs=(vmem(), vmem()),
        compiler_params=params(),
        cost_estimate=cost(0, 6 * rows.shape[0] * chans),
        name="turn",
    )(rows)


def exchange(x, axes):
    return lax.all_to_all(x, axes, split_axis=0, concat_axis=0, tiled=True)


def local(clip_frames, w_spatial, w_time, cotangent, frame_time):
    count = frame_time.shape[0]
    height, width, chans = clip_frames.shape[2:]
    pixels = height * width
    clips = lax.axis_size("clip")
    groups = lax.axis_size("half") * lax.axis_size("core")
    share = chans // groups
    x = clip_frames.reshape(pixels, chans)

    recv = exchange(spread_call(frame_time, cotangent.reshape(count // 2, -1, chans)), "clip")
    acts, slope = forward_call(x, w_spatial.reshape(3, 3 * chans, chans), width)
    padded_t = jnp.pad(x.T, ((0, 0), (width, width)))
    place = jnp.stack([frame_time[lax.axis_index("clip")], lax.axis_index("core"), jnp.int32(count)])
    hidden_grad, keep, send = filter_call(
        place, recv, slope, acts.T, x.T, padded_t, w_time.transpose(0, 2, 1), width
    )
    w_back = w_spatial[::-1, ::-1].transpose(0, 1, 3, 2).reshape(3, 3 * chans, chans)
    clip_grad = back_call(hidden_grad, w_back, width)

    came = lax.ppermute(send, "core", [(0, 1), (1, 0)])
    depth = keep.shape[0] // (2 * clips)
    parts = (keep + came.astype(F32)).astype(BF16).reshape(2 * clips, depth, chans)
    parts = exchange(parts, ("half", "clip"))
    parts, clip_grad = lax.optimization_barrier((parts, clip_grad))
    factor = 1.0 / math.sqrt(clip_frames.shape[0] * groups * count * pixels)
    rows = exchange(total_call(parts, factor, clips), "clip")
    ws, wt = turn_call(rows.reshape(clips * depth, chans), share)
    ws = ws.reshape(3, 3, share, chans).transpose(0, 1, 3, 2)
    return (clip_grad.reshape(clip_frames.shape), ws, wt.transpose(0, 2, 1))


def solution(mesh):
    clips, groups = mesh.devices.shape
    parts = Mesh(mesh.devices.reshape(clips, 2, groups // 2), ("clip", "half", "core"))
    group = ("half", "core")
    return jax.shard_map(
        local,
        mesh=parts,
        in_specs=(
            P(group, "clip", None, None, None),
            P(),
            P(),
            P(group, None, "clip", None, None),
            P(),
        ),
        out_specs=(
            P(group, "clip", None, None, None),
            P(None, None, None, group),
            P(None, None, group),
        ),
        check_vma=False,
    )
```
